256 devices in a mesh: seq: 32 (over y, x, core), tensor: 8 (over z).
Axes of the slice: x: 4, y: 4, z: 8, core: 2. Of those that a mesh axis runs over, the one named last changes fastest.
Arguments:
- tokens: bfloat16 [65536, 5120], P('seq', 'tensor'), may hold values from -6 to 6
- value_weight: bfloat16 [5120, 1024], P('tensor'), may hold values from -0.125 to 0.125
- adapter_down_maps: bfloat16 [128, 32, 5120], P('seq', None, 'tensor'), may hold values from -0.078125 to 0.078125
- adapter_up_maps: bfloat16 [128, 32, 1024], P('seq', None, 'tensor'), may hold values from -1 to 1
- adapter_of_tile: int32 [512], P('seq'), may hold values from 0 to 127, as said below
- cotangent: bfloat16 [65536, 1024], P('seq', 'tensor'), may hold values from -6 to 6
Outputs:
- value: bfloat16 [65536, 1024], P('seq', 'tensor')
- grad_down: float32 [128, 32, 5120], P('seq', None, 'tensor')
- up_gradient: float32 [128, 32, 1024], P('seq', None, 'tensor')
The draws below stay inside these ranges and needn't reach their ends.
Inputs may be any that keep to these rules, and one draw needn't show every extreme that they name: `adapter_of_tile`: owner of a tile is its adapter // 4. Within the aligned blocks of 2048 // 128 tiles (the tiles of one device), no owner takes more than 2 tiles; in every block some owner takes exactly 2, and one owner takes 2 tiles from every block.
All inputs are finite; a program needn't handle non-finite values.
Results may differ from the reference program's by a relative error of at most 0.0053.
Values may be sent and summed in bfloat16 or wider, within the bound.
A program may use at most 128 MiB of HBM per device.

```python
import jax
import jax.numpy as jnp
from jax import lax

MODEL_WIDTH = 5120
VALUE_WIDTH = 1024
ADAPTER_RANK = 32
TILE = 128
CAP = 2
ADAPT_DEV = 4
TOK_DEV = 2048
TOKENS = 65536
ADAPTER_COUNT = 128
N_SEQ = 32


def draw_adapter_of_tile(key, part):
    key = jax.random.fold_in(key, 11)
    key_heat, key_forced, key_noise, key_local = jax.random.split(key, 4)
    total_slots = N_SEQ * CAP
    slot_owner = jnp.arange(total_slots, dtype=jnp.int32) // CAP
    heat = jax.random.randint(key_heat, (N_SEQ,), 0, 4)
    forced = jax.random.randint(key_forced, (), 0, N_SEQ)
    noise = jax.random.randint(key_noise, (N_SEQ, total_slots), 0, 2 ** 14)
    score = noise - heat[slot_owner][None, :] * 2 ** 12 - (slot_owner == forced).astype(jnp.int32)[None, :] * 2 ** 16
    score = score * total_slots + jnp.arange(total_slots, dtype=jnp.int32)[None, :]
    chosen = jnp.argsort(score, axis=1, stable=True)[:, :TOK_DEV // TILE]
    owners = chosen // CAP
    local = jax.random.randint(key_local, owners.shape, 0, ADAPT_DEV)
    return (owners * ADAPT_DEV + local).reshape(-1).astype(jnp.int32)


def spiked(drawn, stream_key, source, target, shards_of, factor):
    def block_of(dim):
        return (jnp.arange(drawn.shape[dim]) // (drawn.shape[dim] // shards_of)).reshape((-1,) + (1,) * (drawn.ndim - 1 - dim))

    first = jax.random.permutation(stream_key, shards_of)[block_of(target)]
    second = (block_of(target) + shards_of // 2) % shards_of
    return jnp.where((block_of(source) == first) | (block_of(source) == second), factor * drawn, drawn)


def levels(own_key, extent, cuts, smallest, high):
    def one(dim, blocks):
        heights = jax.random.uniform(jax.random.fold_in(jax.random.fold_in(own_key, 6), dim), (blocks,), jnp.float32, smallest / len(cuts), high / len(cuts))
        return jnp.repeat(jnp.exp(heights), extent[dim] // blocks).reshape((-1,) + (1,) * (len(extent) - dim - 1))

    loudness = one(*cuts[0])
    for cut in cuts[1:]:
        loudness = loudness * one(*cut)
    return loudness


def scatter_about(own_key, shape, spread, reach, cuts=(), kind=jnp.bfloat16):
    entries = spread * jax.random.normal(own_key, shape, jnp.float32)
    if cuts:
        entries = entries * levels(own_key, shape, cuts, -0.22, 0.18)
    return jnp.clip(entries, -reach, reach).astype(kind)


def gaussian_with(key, dims, spread, limit, pieces, heavy, kind=jnp.bfloat16):
    drawn = spread * jax.random.normal(key, dims, jnp.float32)
    if pieces:
        drawn = drawn * levels(key, dims, pieces, -0.22, 0.18)
    return jnp.clip(spiked(drawn, jax.random.fold_in(key, 3), *heavy), -limit, limit).astype(kind)


def setup_inputs(seed: int = 0) -> dict:
    arg_keys = jax.random.split(jax.random.key(seed), 7)
    tokens = scatter_about(arg_keys[0], (TOKENS, MODEL_WIDTH), 1.0, 6.0, ((0, 32), (1, 8)))
    value_weight = gaussian_with(arg_keys[1], (MODEL_WIDTH, VALUE_WIDTH), MODEL_WIDTH ** -0.5, 0.125, ((0, 8),), (0, 1, 8, 2.0))
    adapter_down_maps = scatter_about(arg_keys[2], (ADAPTER_COUNT, ADAPTER_RANK, MODEL_WIDTH), MODEL_WIDTH ** -0.5, 0.078125, ((0, 32), (2, 8)))
    adapter_up_maps = scatter_about(arg_keys[3], (ADAPTER_COUNT, ADAPTER_RANK, VALUE_WIDTH), ADAPTER_RANK ** -0.5, 1.0, ((0, 32), (2, 8)))
    adapter_of_tile = draw_adapter_of_tile(jax.random.fold_in(arg_keys[6], 71), 0)
    cotangent = scatter_about(arg_keys[5], (TOKENS, VALUE_WIDTH), 1.0, 6.0, ((0, 32), (1, 8)))
    return {"tokens": tokens, "value_weight": value_weight, "adapter_down_maps": adapter_down_maps, "adapter_up_maps": adapter_up_maps, "adapter_of_tile": adapter_of_tile, "cotangent": cotangent}


adapter_scale = 2.0


def reference(tokens, value_weight, adapter_down_maps, adapter_up_maps, adapter_of_tile, cotangent):
    frozen_output = jnp.dot(tokens, value_weight, preferred_element_type=jnp.float32)
    count = tokens.shape[0] // TILE
    x_tiles = tokens.reshape(count, TILE, MODEL_WIDTH)
    g_tiles = cotangent.reshape(count, TILE, VALUE_WIDTH)

    def visit(carry, inputs):
        acc_down, up_accumulator = carry
        x_block, gradient_block, identity_matrix = inputs
        down_matrix = lax.dynamic_index_in_dim(adapter_down_maps, identity_matrix, 0, keepdims=False)
        up_matrix = lax.dynamic_index_in_dim(adapter_up_maps, identity_matrix, 0, keepdims=False)
        lowrank_state = jnp.dot(x_block, down_matrix.T, preferred_element_type=jnp.float32).astype(jnp.bfloat16)
        gradient_lowrank = (adapter_scale * jnp.dot(gradient_block, up_matrix.T, preferred_element_type=jnp.float32)).astype(jnp.bfloat16)
        adapter_update = (adapter_scale * jnp.dot(lowrank_state, up_matrix, preferred_element_type=jnp.float32)).astype(jnp.bfloat16)
        acc_down = acc_down.at[identity_matrix].add(jnp.dot(gradient_lowrank.T, x_block, preferred_element_type=jnp.float32))
        up_accumulator = up_accumulator.at[identity_matrix].add(adapter_scale * jnp.dot(lowrank_state.T, gradient_block, preferred_element_type=jnp.float32))
        return (acc_down, up_accumulator), adapter_update

    start = (jnp.zeros((ADAPTER_COUNT, ADAPTER_RANK, MODEL_WIDTH), jnp.float32), jnp.zeros((ADAPTER_COUNT, ADAPTER_RANK, VALUE_WIDTH), jnp.float32))
    (grad_down, up_gradient), deltas = lax.scan(visit, start, (x_tiles, g_tiles, adapter_of_tile))
    value = (frozen_output + deltas.reshape(-1, VALUE_WIDTH).astype(jnp.float32)).astype(jnp.bfloat16)
    return value, grad_down, up_gradient
```

```python
import jax
import jax.numpy as jnp
from jax import lax
from jax.sharding import PartitionSpec as P

TILE = 128
adapter_scale = 2.0


def body(tokens, value_weight, adapter_down_maps, adapter_up_maps, adapter_of_tile, cotangent):
    token_rows, width_part = tokens.shape
    feature_portion = cotangent.shape[1]
    tile_count = token_rows // TILE
    adapters = jnp.concatenate([adapter_down_maps, adapter_up_maps], axis=2)
    all_adapters = lax.all_gather(adapters, "seq", axis=0, tiled=True)
    adapter_count = all_adapters.shape[0]
    frozen_output = lax.psum_scatter(
        lax.dot_general(
            tokens, value_weight, (((1,), (0,)), ((), ())), preferred_element_type=jnp.float32
        ).astype(jnp.bfloat16),
        "tensor",
        scatter_dimension=1,
        tiled=True,
    )
    picked = all_adapters[adapter_of_tile]
    selected_down = picked[:, :, :width_part]
    selected_up = picked[:, :, width_part:]
    x_tiles = tokens.reshape(tile_count, TILE, width_part)
    g_tiles = cotangent.reshape(tile_count, TILE, feature_portion)
    low_part = jnp.einsum("std,srd->srt", x_tiles, selected_down, preferred_element_type=jnp.float32)
    glow_part = jnp.einsum("stv,srv->srt", g_tiles, selected_up, preferred_element_type=jnp.float32)
    sums = lax.psum(jnp.concatenate([low_part, glow_part], axis=1), "tensor")
    rank = selected_down.shape[1]
    low = sums[:, :rank].astype(jnp.bfloat16)
    glow = (adapter_scale * sums[:, rank:]).astype(jnp.bfloat16)
    update = (
        adapter_scale * jnp.einsum("srt,srv->stv", low, selected_up, preferred_element_type=jnp.float32)
    ).astype(jnp.bfloat16)
    down_terms = jnp.einsum("srt,std->srd", glow, x_tiles, preferred_element_type=jnp.float32)
    up_terms = adapter_scale * jnp.einsum("srt,stv->srv", low, g_tiles, preferred_element_type=jnp.float32)
    terms = jnp.concatenate([down_terms, up_terms], axis=2)
    summed = jnp.zeros((adapter_count,) + terms.shape[1:], jnp.float32).at[adapter_of_tile].add(terms)
    grads = lax.psum_scatter(summed.astype(jnp.bfloat16), "seq", scatter_dimension=0, tiled=True)
    grads = grads.astype(jnp.float32)
    value = (
        frozen_output.astype(jnp.float32) + update.reshape(token_rows, feature_portion).astype(jnp.float32)
    ).astype(jnp.bfloat16)
    return value, grads[:, :, :width_part], grads[:, :, width_part:]


def solution(mesh):
    in_specs = (
        P("seq", "tensor"),
        P("tensor", None),
        P("seq", None, "tensor"),
        P("seq", None, "tensor"),
        P("seq"),
        P("seq", "tensor"),
    )
    out_specs = (P("seq", "tensor"), P("seq", None, "tensor"), P("seq", None, "tensor"))
    return jax.shard_map(body, mesh=mesh, in_specs=in_specs, out_specs=out_specs, check_vma=False)
```

```python
import jax
import jax.numpy as jnp
from jax import lax
from jax.experimental import pallas as pl
from jax.experimental.pallas import tpu as pltpu
from jax.sharding import PartitionSpec as P

TILE = 128
NX, NY, NC, NZ = 4, 4, 2, 8
OWN = 4
SCALE = 2.0
SUB = 2
BLK = 256
MESH = pl.DeviceIdType.MESH
BF = jnp.bfloat16
F32 = jnp.float32


def kernel(
    ids, tok_h, w_h, down_h, up_h, cot_h,
    val_o, gd_o, ug_o,
    tok, w, cot, ad, acc, zs, zr, part, ar, low, tfull, tpart, tab, tabp, tabs,
    g, r1, r2, sf, sb, r3, r4, fin, rfin, full,
    lsem, ag_s, ag_r, d_s, d_r, z_s, z_r, ar_s, ar_r, br_s, br_r, t_s, t_r, g_s, g_r, f_s, f_r,
):
    width = tok.shape[1]
    rows = tok.shape[0]
    rank = down_h.shape[1]
    feat = cot.shape[1]
    tiles = rows // TILE
    cols = width + feat
    half = cols // 2
    hrows = rows // 2
    srows = hrows // SUB
    s_idx = lax.axis_index("seq")
    z = lax.axis_index("tensor")
    c = s_idx % 2
    x = (s_idx // 2) % NX
    y = s_idx // (2 * NX)

    def dev(yy, xx, cc):
        return ((yy * NX + xx) * NC + cc, z)

    def zdev(d):
        return (s_idx, (z + d) % NZ)

    pos = ((y, x), (x, y))

    def hdev(h, dp, dq):
        pp, qq = (pos[h][0] + dp + 4) % 4, (pos[h][1] + dq + 4) % 4
        return dev(pp, qq, c) if h == 0 else dev(qq, pp, c)

    mate = dev(y, x, 1 - c)

    def remote(src, dst, ss, rs, device):
        return pltpu.make_async_remote_copy(
            src_ref=src, dst_ref=dst, send_sem=ss, recv_sem=rs, device_id=device, device_id_type=MESH
        )

    sent = []

    def send(src, dst, ss, rs, device):
        cp = remote(src, dst, ss, rs, device)
        cp.start()
        sent.append(cp)

    def got(dst, ss, rs, device):
        remote(dst, dst, ss, rs, device).wait_recv()

    loads = []
    for h in range(2):
        own = ad.at[h, c, pos[h][0], pos[h][1]]
        loads.append(pltpu.make_async_copy(down_h.at[pl.ds(2 * h, 2)], own.at[:, :, pl.ds(0, width)], lsem.at[2 * h]))
        loads.append(pltpu.make_async_copy(up_h.at[pl.ds(2 * h, 2)], own.at[:, :, pl.ds(width, feat)], lsem.at[2 * h + 1]))
    loads.append(pltpu.make_async_copy(tok_h, tok, lsem.at[4]))
    loads.append(pltpu.make_async_copy(w_h, w, lsem.at[5]))
    loads.append(pltpu.make_async_copy(cot_h, cot, lsem.at[6]))
    for cp in loads:
        cp.start()
    bar = pltpu.get_barrier_semaphore()
    friends = [zdev(d) for d in range(1, NZ)] + [mate]
    friends += [hdev(0, 1, 0), hdev(0, -1, 0), hdev(0, 0, 1), hdev(0, 0, -1)]
    for f in friends:
        pl.semaphore_signal(bar, inc=1, device_id=f, device_id_type=MESH)
    lane = lax.broadcasted_iota(jnp.int32, (8, 128), 1)
    row = lax.broadcasted_iota(jnp.int32, (8, 128), 0)
    first = jnp.full((8, 128), tiles, jnp.int32)
    count = jnp.zeros((8, 128), jnp.int32)
    last = jnp.full((8, 128), tiles, jnp.int32)
    for t in range(tiles):
        hit = lane == ids[t]
        last = jnp.where(hit & (count == 1), t, last)
        first = jnp.where(hit & (count == 0), t, first)
        count = count + hit.astype(jnp.int32)
    tab[...] = jnp.where(row == 0, first, last)
    tfull[tiles] = jnp.zeros((rank, cols), BF)
    tpart[tiles] = jnp.zeros((rank, half), BF)
    for cp in loads[:4]:
        cp.wait()
    pl.semaphore_wait(bar, len(friends))

    def ag1():
        for h in range(2):
            blk = ad.at[h, c, pos[h][0], pos[h][1]]
            send(blk, blk, ag_s.at[h, 0, 0], ag_r.at[h, 0, 0], hdev(h, 0, 1))
            send(blk, blk, ag_s.at[h, 0, 1], ag_r.at[h, 0, 1], hdev(h, 0, -1))
        send(tab, tabp, t_s.at[1], t_r.at[1], mate)

    def ag2():
        for h in range(2):
            pp, qq = pos[h]
            for i, dq in ((0, 1), (1, -1)):
                prev = (qq - dq + 4) % 4
                blk = ad.at[h, c, pp, prev]
                got(blk, ag_s.at[h, 0, i], ag_r.at[h, 0, i], hdev(h, 0, dq))
                piece = ad.at[h, c, pp, prev, pl.ds(i, 1)]
                send(piece, piece, ag_s.at[h, 1, i], ag_r.at[h, 1, i], hdev(h, 0, dq))

    def ag3():
        for h in range(2):
            pp, qq = pos[h]
            for i, dq in ((0, 1), (1, -1)):
                piece = ad.at[h, c, pp, (qq + 2) % 4, pl.ds(i, 1)]
                got(piece, ag_s.at[h, 1, i], ag_r.at[h, 1, i], hdev(h, 0, dq))
            blk = ad.at[h, c, pp]
            send(blk, blk, ag_s.at[h, 2, 0], ag_r.at[h, 2, 0], hdev(h, 1, 0))
            send(blk, blk, ag_s.at[h, 2, 1], ag_r.at[h, 2, 1], hdev(h, -1, 0))
            send(blk, blk, d_s.at[h, 0], d_r.at[h, 0], mate)

    def ag4():
        for h in range(2):
            pp, qq = pos[h]
            for i, dp in ((0, 1), (1, -1)):
                prev = (pp - dp + 4) % 4
                blk = ad.at[h, c, prev]
                got(blk, ag_s.at[h, 2, i], ag_r.at[h, 2, i], hdev(h, dp, 0))
                piece = ad.at[h, c, prev, pl.ds(2 * i, 2)]
                send(piece, piece, ag_s.at[h, 3, i], ag_r.at[h, 3, i], hdev(h, dp, 0))
                send(blk, blk, d_s.at[h, 1 + i], d_r.at[h, 1 + i], mate)

    def ag5():
        for h in range(2):
            pp, qq = pos[h]
            far = (pp + 2) % 4
            for i, dp in ((0, 1), (1, -1)):
                piece = ad.at[h, c, far, pl.ds(2 * i, 2)]
                got(piece, ag_s.at[h, 3, i], ag_r.at[h, 3, i], hdev(h, dp, 0))
            blk = ad.at[h, c, far]
            send(blk, blk, d_s.at[h, 3], d_r.at[h, 3], mate)

    def ag6():
        for h in range(2):
            pp, qq = pos[h]
            for i, d in enumerate((0, -1, 1, 2)):
                blk = ad.at[h, 1 - c, (pp + d + 4) % 4]
                got(blk, d_s.at[h, i], d_r.at[h, i], mate)

    def zpart(s):
        for i in range(2):
            d = (z + NZ - 1 - s) % NZ if i == 0 else (z + 1 + s) % NZ
            fcol = pl.ds(pl.multiple_of(d * feat, feat), feat)

            def step(r, _):
                a = tok[pl.ds(pl.multiple_of(i * hrows + r * BLK, BLK), BLK), :]
                acc[i, pl.ds(pl.multiple_of(r * BLK, BLK), BLK), :] = jnp.dot(
                    a, w[:, fcol], preferred_element_type=F32
                )
                return 0

            lax.fori_loop(0, hrows // BLK, step, 0)

    def zsend(s):
        for u in range(SUB):
            for i in range(2):
                if s > 0:
                    got(zr.at[i, s - 1, u], z_s.at[i, s - 1, u], z_r.at[i, s - 1, u], zdev(1))

                def step(r, _):
                    rr = pl.ds(pl.multiple_of(r * BLK, BLK), BLK)
                    v = acc[i, pl.ds(pl.multiple_of(u * srows + r * BLK, BLK), BLK), :]
                    if s > 0:
                        v = v + zr[i, s - 1, u, rr, :].astype(F32)
                    zs[i, s, u, rr, :] = v.astype(BF)
                    return 0

                lax.fori_loop(0, srows // BLK, step, 0)
                send(
                    zs.at[i, s, u], zr.at[i, s, u], z_s.at[i, s, u], z_r.at[i, s, u],
                    zdev(1) if i == 0 else zdev(NZ - 1),
                )

    def zlast():
        last_step = NZ - 2
        for u in range(SUB):
            for i in range(2):
                got(zr.at[i, last_step, u], z_s.at[i, last_step, u], z_r.at[i, last_step, u], zdev(1))

                def step(r, _):
                    t = (i * hrows + u * srows) // TILE + r
                    k = adapter(t)
                    rr = pl.ds(pl.multiple_of(r * TILE, TILE), TILE)
                    v = acc[i, pl.ds(pl.multiple_of(u * srows + r * TILE, TILE), TILE), :]
                    v = v + zr[i, last_step, u, rr, :].astype(F32)
                    up = ad[k][:, width:]
                    l = low[t // 2, t % 2, pl.ds(0, rank), :]
                    upd = SCALE * lax.dot_general(l, up, (((0,), (0,)), ((), ())), preferred_element_type=F32)
                    v = v + upd.astype(BF).astype(F32)
                    val_o[pl.ds(pl.multiple_of(t * TILE, TILE), TILE), :] = v.astype(BF)
                    return 0

                lax.fori_loop(0, srows // TILE, step, 0)

    def adapter(t):
        a = ids[t]
        owner = a // OWN
        local = a % OWN
        h = local // 2
        cc = owner % 2
        xx = (owner // 2) % NX
        yy = owner // (2 * NX)
        pp = jnp.where(h == 0, yy, xx)
        qq = jnp.where(h == 0, xx, yy)
        return (h, cc, pp, qq, local % 2)

    def lowpart():
        def step(t, _):
            both = ad[adapter(t)]
            rr = pl.ds(pl.multiple_of(t * TILE, TILE), TILE)
            nt = (((1,), (1,)), ((), ()))
            lo = lax.dot_general(both[:, :width], tok[rr, :], nt, preferred_element_type=F32)
            gl = lax.dot_general(both[:, width:], cot[rr, :], nt, preferred_element_type=F32)
            part[t // 2, t % 2, pl.ds(0, rank), :] = lo.astype(BF)
            part[t // 2, t % 2, pl.ds(rank, rank), :] = gl.astype(BF)
            return 0

        lax.fori_loop(0, tiles, step, 0)

    def arsend():
        for d in range(1, NZ):
            to = (z + d) % NZ
            send(part.at[to], ar.at[d], ar_s.at[d], ar_r.at[d], zdev(d))

    def arsum():
        for d in range(1, NZ):
            got(ar.at[d], ar_s.at[d], ar_r.at[d], zdev(d))
        tot = part[z].astype(F32)
        for d in range(1, NZ):
            tot = tot + ar[d].astype(F32)
        low[z, :, pl.ds(0, rank), :] = tot[:, :rank].astype(BF)
        low[z, :, pl.ds(rank, rank), :] = (SCALE * tot[:, rank:]).astype(BF)
        for d in range(1, NZ):
            send(low.at[z], low.at[z], br_s.at[d], br_r.at[d], zdev(d))

    def argot():
        for d in range(1, NZ):
            got(low.at[(z + NZ - d) % NZ], br_s.at[d], br_r.at[d], zdev(d))

    def terms():
        def step(t, _):
            rr = pl.ds(pl.multiple_of(t * TILE, TILE), TILE)
            lo = low[t // 2, t % 2, pl.ds(0, rank), :]
            gl = low[t // 2, t % 2, pl.ds(rank, rank), :]
            tfull[t, :, pl.ds(0, width)] = jnp.dot(gl, tok[rr, :], preferred_element_type=F32).astype(BF)
            tfull[t, :, pl.ds(width, feat)] = (
                SCALE * jnp.dot(lo, cot[rr, :], preferred_element_type=F32)
            ).astype(BF)
            return 0

        lax.fori_loop(0, tiles, step, 0)

    mine = pl.ds(pl.multiple_of(c * half, 128), half)
    theirs = pl.ds(pl.multiple_of((1 - c) * half, 128), half)

    def tsend():
        send(
            tfull.at[pl.ds(0, tiles), :, theirs], tpart.at[pl.ds(0, tiles)], t_s.at[0], t_r.at[0], mate
        )

    def tables():
        cp = pltpu.make_async_copy(tab, tabs.at[0], lsem.at[7])
        cp.start()
        cp.wait()
        got(tabp, t_s.at[1], t_r.at[1], mate)
        cp = pltpu.make_async_copy(tabp, tabs.at[1], lsem.at[8])
        cp.start()
        cp.wait()

    def build(h, pp):
        def step(n, _):
            qq, cc, k = n // 4, (n // 2) % 2, n % 2
            yy, xx = (pp, qq) if h == 0 else (qq, pp)
            a = ((yy * NX + xx) * NC + cc) * OWN + 2 * h + k
            v = tfull[tabs[0, 0, a], :, mine].astype(F32) + tfull[tabs[0, 1, a], :, mine].astype(F32)
            v = v + tpart[tabs[1, 0, a]].astype(F32)
            v = v + tpart[tabs[1, 1, a]].astype(F32)
            g[h, pp, qq, cc, k] = v.astype(BF)
            return 0

        lax.fori_loop(0, 16, step, 0)

    def plus(h, i):
        return (pos[h][0] + 1) % 4 if i == 0 else (pos[h][0] + 3) % 4

    DIRS = ((0, 1), (1, -1))

    def rs1():
        for h in range(2):
            far = (pos[h][0] + 2) % 4
            build(h, far)
            for i, dp in DIRS:
                send(g.at[h, far, pl.ds(2 * i, 2)], r1.at[h, i], g_s.at[h, 0, i], g_r.at[h, 0, i], hdev(h, dp, 0))
        for h in range(2):
            for i, dp in DIRS:
                near = plus(h, i)
                build(h, near)
                raw = pl.ds(2 * (1 - i), 2)
                send(g.at[h, near, raw], r2.at[h, i, raw], g_s.at[h, 1, i], g_r.at[h, 1, i], hdev(h, dp, 0))

    def rs2():
        for h in range(2):
            for i, dp in DIRS:
                near = plus(h, i)
                got(r1.at[h, i], g_s.at[h, 0, i], g_r.at[h, 0, i], hdev(h, dp, 0))

                def step(n, _):
                    qq, cc = n // 2, n % 2
                    g[h, near, 2 * i + qq, cc] = (
                        g[h, near, 2 * i + qq, cc].astype(F32) + r1[h, i, qq, cc].astype(F32)
                    ).astype(BF)
                    return 0

                lax.fori_loop(0, 4, step, 0)
                summed = pl.ds(2 * i, 2)
                send(g.at[h, near, summed], r2.at[h, i, summed], g_s.at[h, 2, i], g_r.at[h, 2, i], hdev(h, dp, 0))

    def rs3():
        for h in range(2):
            build(h, pos[h][0])

    def rs4():
        for h in range(2):
            pp, qq0 = pos[h]
            for i, dp in DIRS:
                raw, summed = pl.ds(2 * (1 - i), 2), pl.ds(2 * i, 2)
                got(r2.at[h, i, raw], g_s.at[h, 1, i], g_r.at[h, 1, i], hdev(h, dp, 0))
                got(r2.at[h, i, summed], g_s.at[h, 2, i], g_r.at[h, 2, i], hdev(h, dp, 0))

            def step(n, _):
                qq, cc = n // 2, n % 2
                v = g[h, pp, qq, cc].astype(F32) + r2[h, 0, qq, cc].astype(F32) + r2[h, 1, qq, cc].astype(F32)
                sf[h, qq, cc] = v
                sb[h, qq, cc] = v.astype(BF)
                return 0

            lax.fori_loop(0, 8, step, 0)
            far = (qq0 + 2) % 4
            for i, dq in DIRS:
                near = (qq0 + dq + 4) % 4
                send(sb.at[h, far, i], r3.at[h, i], g_s.at[h, 3, i], g_r.at[h, 3, i], hdev(h, 0, dq))
                send(sb.at[h, near, 1 - i], r4.at[h, i, 1 - i], g_s.at[h, 4, i], g_r.at[h, 4, i], hdev(h, 0, dq))

    def rs5():
        for h in range(2):
            qq0 = pos[h][1]
            for i, dq in DIRS:
                near = (qq0 + dq + 4) % 4
                got(r3.at[h, i], g_s.at[h, 3, i], g_r.at[h, 3, i], hdev(h, 0, dq))
                sb[h, near, i] = (sf[h, near, i] + r3[h, i].astype(F32)).astype(BF)
                send(sb.at[h, near, i], r4.at[h, i, i], g_s.at[h, 5, i], g_r.at[h, 5, i], hdev(h, 0, dq))

    def rs6():
        for h in range(2):
            qq0 = pos[h][1]
            for i, dq in DIRS:
                got(r4.at[h, i, 1 - i], g_s.at[h, 4, i], g_r.at[h, 4, i], hdev(h, 0, dq))
                got(r4.at[h, i, i], g_s.at[h, 5, i], g_r.at[h, 5, i], hdev(h, 0, dq))
            for cc in range(2):
                fin[h, cc] = sf[h, qq0, cc] + r4[h, 0, cc].astype(F32) + r4[h, 1, cc].astype(F32)
            send(fin.at[h, 1 - c], rfin.at[h], f_s.at[h], f_r.at[h], mate)
            full[pl.ds(2 * h, 2), :, mine] = fin[h, c]
        for h in range(2):
            got(rfin.at[h], f_s.at[h], f_r.at[h], mate)
            full[pl.ds(2 * h, 2), :, theirs] = rfin[h]
        gd_o[...] = full[:, :, :width]
        ug_o[...] = full[:, :, width:]

    ag1()
    loads[4].wait()
    loads[5].wait()
    zpart(0)
    zsend(0)
    ag2()
    zpart(1)
    ag3()
    zsend(1)
    zpart(2)
    zsend(2)
    ag4()
    zpart(3)
    zsend(3)
    ag5()
    zpart(4)
    loads[6].wait()
    tables()
    ag6()
    lowpart()
    arsend()
    zsend(4)
    arsum()
    zpart(5)
    zsend(5)
    argot()
    terms()
    tsend()
    zpart(6)
    got(tpart.at[pl.ds(0, tiles)], t_s.at[0], t_r.at[0], mate)
    rs1()
    zsend(6)
    rs2()
    rs3()
    zpart(7)
    rs4()
    zlast()
    rs5()
    rs6()
    for cp in sent:
        cp.wait_send()


def body(tokens, value_weight, adapter_down_maps, adapter_up_maps, adapter_of_tile, cotangent):
    rows, width = tokens.shape
    feat = cotangent.shape[1]
    own, rank, _ = adapter_down_maps.shape
    tiles = rows // TILE
    cols = width + feat
    half = cols // 2
    hrows = rows // 2
    srows = hrows // SUB
    dma = pltpu.SemaphoreType.DMA
    vm = pltpu.VMEM
    any_spec = pl.BlockSpec(memory_space=pl.ANY)
    vmem = pl.BlockSpec(memory_space=pltpu.VMEM)
    return pl.pallas_call(
        kernel,
        out_shape=(
            jax.ShapeDtypeStruct((rows, feat), BF),
            jax.ShapeDtypeStruct((own, rank, width), F32),
            jax.ShapeDtypeStruct((own, rank, feat), F32),
        ),
        in_specs=[pl.BlockSpec(memory_space=pltpu.SMEM)] + [any_spec] * 5,
        out_specs=(vmem, vmem, vmem),
        scratch_shapes=[
            vm((rows, width), BF),
            vm(value_weight.shape, BF),
            vm((rows, feat), BF),
            vm((2, NC, 4, 4, 2, rank, cols), BF),
            vm((2, hrows, feat), F32),
            vm((2, NZ - 1, SUB, srows, feat), BF),
            vm((2, NZ - 1, SUB, srows, feat), BF),
            vm((NZ, tiles // NZ, 2 * rank, TILE), BF),
            vm((NZ, tiles // NZ, 2 * rank, TILE), BF),
            vm((NZ, tiles // NZ, 2 * rank, TILE), BF),
            vm((tiles + 1, rank, cols), BF),
            vm((tiles + 1, rank, half), BF),
            vm((8, 128), jnp.int32),
            vm((8, 128), jnp.int32),
            pltpu.SMEM((2, 8, 128), jnp.int32),
            vm((2, 4, 4, 2, 2, rank, half), BF),
            vm((2, 2, 2, 2, 2, rank, half), BF),
            vm((2, 2, 4, 2, 2, rank, half), BF),
            vm((2, 4, 2, 2, rank, half), F32),
            vm((2, 4, 2, 2, rank, half), BF),
            vm((2, 2, 2, rank, half), BF),
            vm((2, 2, 2, 2, rank, half), BF),
            vm((2, 2, 2, rank, half), F32),
            vm((2, 2, rank, half), F32),
            vm((own, rank, cols), F32),
            dma((9,)),
            dma((2, 4, 2)),
            dma((2, 4, 2)),
            dma((2, 4)),
            dma((2, 4)),
            dma((2, NZ - 1, SUB)),
            dma((2, NZ - 1, SUB)),
            dma((NZ,)),
            dma((NZ,)),
            dma((NZ,)),
            dma((NZ,)),
            dma((2,)),
            dma((2,)),
            dma((2, 6, 2)),
            dma((2, 6, 2)),
            dma((2,)),
            dma((2,)),
        ],
        compiler_params=pltpu.CompilerParams(
            collective_id=0, has_side_effects=True, vmem_limit_bytes=56 * 2**20
        ),
        name="adapters_and_projection",
    )(adapter_of_tile, tokens, value_weight, adapter_down_maps, adapter_up_maps, cotangent)


def solution(mesh):
    in_specs = (
        P("seq", "tensor"),
        P("tensor", None),
        P("seq", None, "tensor"),
        P("seq", None, "tensor"),
        P("seq"),
        P("seq", "tensor"),
    )
    out_specs = (P("seq", "tensor"), P("seq", None, "tensor"), P("seq", None, "tensor"))
    return jax.shard_map(body, mesh=mesh, in_specs=in_specs, out_specs=out_specs, check_vma=False)
```

```python
import jax
import jax.numpy as jnp
from jax import lax
from jax.experimental import pallas as pl
from jax.experimental.pallas import tpu as pltpu
from jax.sharding import PartitionSpec as P

TILE = 128
NX, NY, NC, NZ = 4, 4, 2, 8
OWN = 4
SCALE = 2.0
SUB = 2
BLK = 256
UN = 4
MESH = pl.DeviceIdType.MESH
BF = jnp.bfloat16
F32 = jnp.float32
DIRS = ((0, 1), (1, -1))
UP, DOWN = 0, 1
ALL_Q = ((0, 4),)
TWO_Q = ((0, 2), (2, 2))


def kernel(
    ids, tok_h, w_h, down_h, up_h, cot_h,
    val_o, gd_o, ug_o,
    tok, w, cot, adu, add, acc, zs, zr, part, ar, low, tu, td, tpu, tpd, tab, tabp, tabs, place_of,
    gu, gd, r1u, r1d, r2u, r2d, sfu, sfd, sbu, sbd, r3u, r3d, r4u, r4d, finu, find, rfu, rfd,
    lsem, ag_s, ag_r, d_s, d_r, z_s, z_r, ar_s, ar_r, br_s, br_r, t_s, t_r,
    g_s, g_r, q_s, q_r, f_s, f_r,
):
    width = tok.shape[1]
    rows = tok.shape[0]
    rank = down_h.shape[1]
    feat = cot.shape[1]
    tiles = rows // TILE
    hrank = rank // 2
    hrows = rows // 2
    srows = hrows // SUB
    ad = (adu, add)
    tt = (tu, td)
    tp = (tpu, tpd)
    g = (gu, gd)
    r1 = (r1u, r1d)
    r2 = (r2u, r2d)
    sf = (sfu, sfd)
    sb = (sbu, sbd)
    r3 = (r3u, r3d)
    r4 = (r4u, r4d)
    fin = (finu, find)
    rf = (rfu, rfd)
    out = (ug_o, gd_o)
    s_idx = lax.axis_index("seq")
    z = lax.axis_index("tensor")
    c = s_idx % 2
    x = (s_idx // 2) % NX
    y = s_idx // (2 * NX)
    pos = ((y, x), (x, y))

    def dev(yy, xx, cc):
        return ((yy * NX + xx) * NC + cc, z)

    def zdev(d):
        return (s_idx, (z + d) % NZ)

    def hdev(h, dp, dq):
        pp, qq = (pos[h][0] + dp + 4) % 4, (pos[h][1] + dq + 4) % 4
        return dev(pp, qq, c) if h == 0 else dev(qq, pp, c)

    mate = dev(y, x, 1 - c)

    def remote(src, dst, ss, rs, device):
        return pltpu.make_async_remote_copy(
            src_ref=src, dst_ref=dst, send_sem=ss, recv_sem=rs, device_id=device, device_id_type=MESH
        )

    sent = []

    def send(src, dst, ss, rs, device):
        cp = remote(src, dst, ss, rs, device)
        cp.start()
        sent.append(cp)

    def got(dst, ss, rs):
        remote(dst, dst, ss, rs, mate).wait_recv()

    def slot(h, side, p, q=0, k=0, n=1):
        return pl.ds((((h * 2 + side) * 4 + p) * 4 + q) * 2 + k, n)

    loads = []
    for h in range(2):
        loads.append(pltpu.make_async_copy(up_h.at[pl.ds(2 * h, 2)], adu.at[slot(h, 0, 0, n=2)], lsem.at[2 * h]))
        loads.append(pltpu.make_async_copy(down_h.at[pl.ds(2 * h, 2)], add.at[slot(h, 0, 0, n=2)], lsem.at[2 * h + 1]))
    loads.append(pltpu.make_async_copy(tok_h, tok, lsem.at[4]))
    loads.append(pltpu.make_async_copy(cot_h, cot, lsem.at[5]))
    for j in range(NZ + 1):
        d = (z + NZ - j) % NZ
        loads.append(
            pltpu.make_async_copy(
                w_h.at[:, pl.ds(pl.multiple_of(d * feat, feat), feat)],
                w.at[:, pl.ds(j * feat, feat)],
                lsem.at[8 + j],
            )
        )
    for cp in loads:
        cp.start()
    bar = pltpu.get_barrier_semaphore()
    friends = [zdev(d) for d in range(1, NZ)] + [mate]
    friends += [hdev(0, 1, 0), hdev(0, -1, 0), hdev(0, 0, 1), hdev(0, 0, -1)]
    for f in friends:
        pl.semaphore_signal(bar, inc=1, device_id=f, device_id_type=MESH)
    lane = lax.broadcasted_iota(jnp.int32, (8, 128), 1)
    lane_h = lane // 64
    lane_p = (lane // 16) % 4
    lane_q = (lane // 2) % 4
    lane_q = jnp.where(lane_q == 0, 2, jnp.where(lane_q == 1, 1, jnp.where(lane_q == 2, 3, 0)))
    lane_y = (y + jnp.where(lane_h == 0, lane_p, lane_q)) % 4
    lane_x = (x + jnp.where(lane_h == 0, lane_q, lane_p)) % 4
    lane_c = (lane // 8 + c) % 2
    named = ((lane_y * NX + lane_x) * NC + lane_c) * OWN + 2 * lane_h + lane % 2
    row = lax.broadcasted_iota(jnp.int32, (8, 128), 0)
    first = jnp.full((8, 128), tiles, jnp.int32)
    count = jnp.zeros((8, 128), jnp.int32)
    last = jnp.full((8, 128), tiles, jnp.int32)
    for t in range(tiles):
        hit = named == ids[t]
        last = jnp.where(hit & (count == 1), t, last)
        first = jnp.where(hit & (count == 0), t, first)
        count = count + hit.astype(jnp.int32)
    tab[...] = jnp.where(row == 0, first, last)
    for e in range(2):
        tt[e][tiles] = jnp.zeros(tt[e].shape[1:], BF)
        tp[e][tiles] = jnp.zeros(tp[e].shape[1:], BF)
    for t in range(tiles):
        a = ids[t]
        owner = a // OWN
        h = (a % OWN) // 2
        xx = (owner // 2 + NX - x) % NX
        yy = (owner // (2 * NX) + NY - y) % NY
        pq = jnp.where(h == 0, yy * 4 + xx, xx * 4 + yy)
        place_of[t] = ((h * 2 + (owner + c) % 2) * 16 + pq) * 2 + a % 2
    for cp in loads[:4]:
        cp.wait()
    pl.semaphore_wait(bar, len(friends))

    def ag1(e):
        for h in range(2):
            own = ad[e].at[slot(h, 0, 0, n=2)]
            for i, dq in DIRS:
                send(own, ad[e].at[slot(h, 0, 0, 3 - 2 * i, n=2)], ag_s.at[e, h, 0, i], ag_r.at[e, h, 0, i], hdev(h, 0, dq))

    def ag1p(e):
        for h in range(2):
            own = ad[e].at[slot(h, 0, 0, n=2)]
            for i, dp in DIRS:
                send(own, ad[e].at[slot(h, 0, 3 - 2 * i, n=2)], ag_s.at[e, h, 4, i], ag_r.at[e, h, 4, i], hdev(h, dp, 0))

    def ag2(e):
        for h in range(2):
            for i, dq in DIRS:
                near = 3 - 2 * i
                got(ad[e].at[slot(h, 0, 0, near, n=2)], ag_s.at[e, h, 0, i], ag_r.at[e, h, 0, i])
                send(
                    ad[e].at[slot(h, 0, 0, near, i)], ad[e].at[slot(h, 0, 0, 2, i)],
                    ag_s.at[e, h, 1, i], ag_r.at[e, h, 1, i], hdev(h, 0, dq),
                )

    def ag3(e):
        for h in range(2):
            for i, dq in DIRS:
                got(ad[e].at[slot(h, 0, 0, 2, i)], ag_s.at[e, h, 1, i], ag_r.at[e, h, 1, i])
            for i, dp in DIRS:
                send(
                    ad[e].at[slot(h, 0, 0, 1, n=6)], ad[e].at[slot(h, 0, 3 - 2 * i, 1, n=6)],
                    ag_s.at[e, h, 2, i], ag_r.at[e, h, 2, i], hdev(h, dp, 0),
                )
            send(ad[e].at[slot(h, 0, 0, n=8)], ad[e].at[slot(h, 1, 0, n=8)], d_s.at[e, h, 0], d_r.at[e, h, 0], mate)

    def ag4(e):
        for h in range(2):
            for i, dp in DIRS:
                near = 3 - 2 * i
                got(ad[e].at[slot(h, 0, near, n=2)], ag_s.at[e, h, 4, i], ag_r.at[e, h, 4, i])
                got(ad[e].at[slot(h, 0, near, 1, n=6)], ag_s.at[e, h, 2, i], ag_r.at[e, h, 2, i])
                send(
                    ad[e].at[slot(h, 0, near, 2 * i, n=4)], ad[e].at[slot(h, 0, 2, 2 * i, n=4)],
                    ag_s.at[e, h, 3, i], ag_r.at[e, h, 3, i], hdev(h, dp, 0),
                )
                send(ad[e].at[slot(h, 0, near, n=8)], ad[e].at[slot(h, 1, near, n=8)], d_s.at[e, h, near], d_r.at[e, h, near], mate)

    def ag5(e):
        for h in range(2):
            for i, dp in DIRS:
                got(ad[e].at[slot(h, 0, 2, 2 * i, n=4)], ag_s.at[e, h, 3, i], ag_r.at[e, h, 3, i])
            send(ad[e].at[slot(h, 0, 2, n=8)], ad[e].at[slot(h, 1, 2, n=8)], d_s.at[e, h, 2], d_r.at[e, h, 2], mate)

    def ag6(e):
        for h in range(2):
            for j in range(4):
                got(ad[e].at[slot(h, 1, j, n=8)], d_s.at[e, h, j], d_r.at[e, h, j])

    def zpart(m):
        for i in range(2):
            start = (2 * m + 1) * feat if i == 0 else (6 - 2 * m) * feat

            def step(r, _):
                rr = pl.ds(pl.multiple_of(r * BLK, BLK), BLK)
                a = tok[pl.ds(pl.multiple_of(i * hrows + r * BLK, BLK), BLK), :]
                v = jnp.dot(a, w[:, start : start + 2 * feat], preferred_element_type=F32)
                acc[m % 2, i, i, rr, :] = v[:, :feat]
                acc[m % 2, i, 1 - i, rr, :] = v[:, feat:]
                return 0

            lax.fori_loop(0, hrows // BLK, step, 0)

    def zsend(s, u):
        for i in range(2):
            if s > 0:
                got(zr.at[i, s - 1, u], z_s.at[i, s - 1, u], z_r.at[i, s - 1, u])

            def step(r, _):
                rr = pl.ds(pl.multiple_of(r * 128, 128), 128)
                v = acc[(s // 2) % 2, i, s % 2, pl.ds(pl.multiple_of(u * srows + r * 128, 128), 128), :]
                if s > 0:
                    v = v + zr[i, s - 1, u, rr, :].astype(F32)
                zs[i, s, u, rr, :] = v.astype(BF)
                return 0

            lax.fori_loop(0, srows // 128, step, 0)
            send(
                zs.at[i, s, u], zr.at[i, s, u], z_s.at[i, s, u], z_r.at[i, s, u],
                zdev(1) if i == 0 else zdev(NZ - 1),
            )

    def zlast():
        last_step = NZ - 2
        for u in range(SUB):
            for i in range(2):
                got(zr.at[i, last_step, u], z_s.at[i, last_step, u], z_r.at[i, last_step, u])

                def step(r, _):
                    t = (i * hrows + u * srows) // TILE + r
                    rr = pl.ds(pl.multiple_of(r * TILE, TILE), TILE)
                    v = acc[1, i, 1, pl.ds(pl.multiple_of(u * srows + r * TILE, TILE), TILE), :]
                    v = v + zr[i, last_step, u, rr, :].astype(F32)
                    upd = SCALE * lax.dot_general(
                        low[DOWN, t // 2, t % 2], adu[place_of[t]], (((0,), (0,)), ((), ())),
                        preferred_element_type=F32,
                    )
                    v = v + upd.astype(BF).astype(F32)
                    val_o[pl.ds(pl.multiple_of(t * TILE, TILE), TILE), :] = v.astype(BF)
                    return 0

                lax.fori_loop(0, srows // TILE, step, 0, unroll=UN)

    def lowpart(e):
        source = (cot, tok)[e]

        def step(t, _):
            rr = pl.ds(pl.multiple_of(t * TILE, TILE), TILE)
            v = lax.dot_general(
                ad[e][place_of[t]], source[rr, :], (((1,), (1,)), ((), ())), preferred_element_type=F32
            )
            part[e, t // 2, t % 2] = v.astype(BF)
            return 0

        lax.fori_loop(0, tiles, step, 0, unroll=UN)

    ORDER = (4, 3, 5, 2, 6, 1, 7)

    def arsend(e):
        lowpart(e)
        for d in ORDER:
            send(part.at[e, (z + d) % NZ], ar.at[e, d], ar_s.at[e, d], ar_r.at[e, d], zdev(d))

    def arsum(e):
        for d in range(1, NZ):
            got(ar.at[e, d], ar_s.at[e, d], ar_r.at[e, d])
        tot = part[e, z].astype(F32)
        for d in range(1, NZ):
            tot = tot + ar[e, d].astype(F32)
        if e == UP:
            tot = SCALE * tot
        low[e, z] = tot.astype(BF)
        for d in ORDER:
            send(low.at[e, z], low.at[e, z], br_s.at[e, d], br_r.at[e, d], zdev(d))

    def argot(e):
        for d in range(1, NZ):
            got(low.at[e, (z + NZ - d) % NZ], br_s.at[e, d], br_r.at[e, d])

    mine = pl.ds(pl.multiple_of(c * hrank, hrank), hrank)
    theirs = pl.ds(pl.multiple_of((1 - c) * hrank, hrank), hrank)

    def terms(e):
        source = (cot, tok)[e]

        def step(t, _):
            rr = pl.ds(pl.multiple_of(t * TILE, TILE), TILE)
            v = jnp.dot(low[1 - e, t // 2, t % 2], source[rr, :], preferred_element_type=F32)
            if e == UP:
                v = SCALE * v
            tt[e][t] = v.astype(BF)
            return 0

        lax.fori_loop(0, tiles, step, 0, unroll=UN)
        send(tt[e].at[pl.ds(0, tiles), theirs, :], tp[e].at[pl.ds(0, tiles)], t_s.at[e], t_r.at[e], mate)

    def tgot(e):
        got(tp[e].at[pl.ds(0, tiles)], t_s.at[e], t_r.at[e])

    def tables():
        cp = pltpu.make_async_copy(tab, tabs.at[0], lsem.at[6])
        cp.start()
        cp.wait()
        got(tabp, t_s.at[2], t_r.at[2])
        cp = pltpu.make_async_copy(tabp, tabs.at[1], lsem.at[7])
        cp.start()
        cp.wait()

    def build(e, h, rel, group):
        q0, n = group
        base = (h * 4 + rel) * 16
        for cc in range(2):
            here = base + cc * 8 + 2 * q0
            there = base + (1 - cc) * 8 + 2 * q0

            def step(j, _):
                v = tt[e][tabs[0, 0, here + j], mine, :].astype(F32)
                v = v + tt[e][tabs[0, 1, here + j], mine, :].astype(F32)
                v = v + tp[e][tabs[1, 0, there + j]].astype(F32)
                v = v + tp[e][tabs[1, 1, there + j]].astype(F32)
                g[e][h, rel, cc, 2 * q0 + j] = v.astype(BF)
                return 0

            lax.fori_loop(0, 2 * n, step, 0, unroll=min(UN, 2 * n))

    NEAR = (1, 3)

    def rs1far(e, groups, gi):
        q0, n = groups[gi]
        qs = pl.ds(2 * q0, 2 * n)
        for h in range(2):
            build(e, h, 2, groups[gi])
            for i, dp in DIRS:
                send(
                    g[e].at[h, 2, i, qs], r1[e].at[h, i, qs],
                    g_s.at[e, h, gi, 0, i], g_r.at[e, h, gi, 0, i], hdev(h, dp, 0),
                )

    def rs1near(e, groups, gi):
        q0, n = groups[gi]
        qs = pl.ds(2 * q0, 2 * n)
        for h in range(2):
            for i, dp in DIRS:
                build(e, h, NEAR[i], groups[gi])
                send(
                    g[e].at[h, NEAR[i], 1 - i, qs], r2[e].at[h, i, 1 - i, qs],
                    g_s.at[e, h, gi, 1, i], g_r.at[e, h, gi, 1, i], hdev(h, dp, 0),
                )

    def rs2(e, groups, gi):
        q0, n = groups[gi]
        qs = pl.ds(2 * q0, 2 * n)
        for h in range(2):
            for i, dp in DIRS:
                got(r1[e].at[h, i, qs], g_s.at[e, h, gi, 0, i], g_r.at[e, h, gi, 0, i])

                def step(j, _):
                    v = g[e][h, NEAR[i], i, 2 * q0 + j].astype(F32) + r1[e][h, i, 2 * q0 + j].astype(F32)
                    g[e][h, NEAR[i], i, 2 * q0 + j] = v.astype(BF)
                    return 0

                lax.fori_loop(0, 2 * n, step, 0, unroll=UN)
                send(
                    g[e].at[h, NEAR[i], i, qs], r2[e].at[h, i, i, qs],
                    g_s.at[e, h, gi, 2, i], g_r.at[e, h, gi, 2, i], hdev(h, dp, 0),
                )

    def rs3(e):
        for h in range(2):
            build(e, h, 0, (0, 4))

    def rs4(e, groups, gi):
        q0, n = groups[gi]
        qs = pl.ds(2 * q0, 2 * n)
        for h in range(2):
            for i, dp in DIRS:
                got(r2[e].at[h, i, 1 - i, qs], g_s.at[e, h, gi, 1, i], g_r.at[e, h, gi, 1, i])
                got(r2[e].at[h, i, i, qs], g_s.at[e, h, gi, 2, i], g_r.at[e, h, gi, 2, i])
            for cc in range(2):

                def step(j, _):
                    qk = 2 * q0 + j
                    v = g[e][h, 0, cc, qk].astype(F32) + r2[e][h, 0, cc, qk].astype(F32)
                    v = v + r2[e][h, 1, cc, qk].astype(F32)
                    sf[e][h, cc, qk] = v
                    sb[e][h, cc, qk] = v.astype(BF)
                    return 0

                lax.fori_loop(0, 2 * n, step, 0, unroll=UN)
            for i, dq in DIRS:
                if q0 == 0:
                    send(
                        sb[e].at[h, i, pl.ds(0, 2)], r3[e].at[h, i],
                        q_s.at[e, h, 0, i], q_r.at[e, h, 0, i], hdev(h, 0, dq),
                    )
                if q0 <= 1 + i < q0 + n:
                    send(
                        sb[e].at[h, 1 - i, pl.ds(2 + 2 * i, 2)], r4[e].at[h, i, 1 - i],
                        q_s.at[e, h, 1, i], q_r.at[e, h, 1, i], hdev(h, 0, dq),
                    )

    def rs5(e):
        for h in range(2):
            for i, dq in DIRS:
                got(r3[e].at[h, i], q_s.at[e, h, 0, i], q_r.at[e, h, 0, i])
                unit = pl.ds(2 + 2 * i, 2)
                sb[e][h, i, unit] = (sf[e][h, i, unit] + r3[e][h, i].astype(F32)).astype(BF)
                send(
                    sb[e].at[h, i, unit], r4[e].at[h, i, i],
                    q_s.at[e, h, 2, i], q_r.at[e, h, 2, i], hdev(h, 0, dq),
                )

    def rs6(e):
        for h in range(2):
            for i, dq in DIRS:
                got(r4[e].at[h, i, 1 - i], q_s.at[e, h, 1, i], q_r.at[e, h, 1, i])
                got(r4[e].at[h, i, i], q_s.at[e, h, 2, i], q_r.at[e, h, 2, i])
            own = pl.ds(6, 2)
            fin[e][h] = sf[e][h, 1, own] + r4[e][h, 0, 1].astype(F32) + r4[e][h, 1, 1].astype(F32)
            send(fin[e].at[h], rf[e].at[h], f_s.at[e, h], f_r.at[e, h], mate)
            v = sf[e][h, 0, own] + r4[e][h, 0, 0].astype(F32) + r4[e][h, 1, 0].astype(F32)
            out[e][pl.ds(2 * h, 2), mine, :] = v

    def rs7(e):
        for h in range(2):
            got(rf[e].at[h], f_s.at[e, h], f_r.at[e, h])
            out[e][pl.ds(2 * h, 2), theirs, :] = rf[e][h]

    def tabsend():
        send(tab, tabp, t_s.at[2], t_r.at[2], mate)

    def landed(*which):
        for j in which:
            for cp in loads[j:] if j == 6 else loads[j : j + 1]:
                cp.wait()

    plan = (
        (ag1, UP),
        (ag1p, UP),
        (tabsend,),
        (landed, 4, 6),
        (zpart, 0),
        (zsend, 0, 0),
        (zsend, 0, 1),
        (ag2, UP),
        (ag1, DOWN),
        (landed, 5),
        (tables,),
        (ag3, UP),
        (ag1p, DOWN),
        (ag4, UP),
        (zsend, 1, 0),
        (ag2, DOWN),
        (zsend, 1, 1),
        (ag5, UP),
        (ag3, DOWN),
        (zpart, 1),
        (ag6, UP),
        (arsend, UP),
        (zsend, 2, 0),
        (zsend, 2, 1),
        (ag4, DOWN),
        (arsum, UP),
        (zsend, 3, 0),
        (zpart, 2),
        (zsend, 3, 1),
        (argot, UP),
        (terms, DOWN),
        (ag5, DOWN),
        (zsend, 4, 0),
        (tgot, DOWN),
        (rs1far, DOWN, TWO_Q, 0),
        (zsend, 4, 1),
        (ag6, DOWN),
        (arsend, DOWN),
        (rs1far, DOWN, TWO_Q, 1),
        (rs1near, DOWN, TWO_Q, 0),
        (zsend, 5, 0),
        (rs1near, DOWN, TWO_Q, 1),
        (zsend, 5, 1),
        (arsum, DOWN),
        (zpart, 3),
        (rs2, DOWN, TWO_Q, 0),
        (rs2, DOWN, TWO_Q, 1),
        (zsend, 6, 0),
        (zsend, 6, 1),
        (rs3, DOWN),
        (argot, DOWN),
        (terms, UP),
        (rs4, DOWN, TWO_Q, 0),
        (tgot, UP),
        (rs1far, UP, ALL_Q, 0),
        (rs1near, UP, ALL_Q, 0),
        (rs4, DOWN, TWO_Q, 1),
        (rs3, UP),
        (rs2, UP, ALL_Q, 0),
        (rs5, DOWN),
        (zlast,),
        (rs4, UP, ALL_Q, 0),
        (rs6, DOWN),
        (rs5, UP),
        (rs7, DOWN),
        (rs6, UP),
        (rs7, UP),
    )
    for act, *details in plan:
        act(*details)
    for cp in sent:
        cp.wait_send()


def place(val_i, gd_i, ug_i, val_o, gd_o, ug_o):
    val_o[...] = val_i[...]
    gd_o[...] = gd_i[...]
    ug_o[...] = ug_i[...]


def body(tokens, value_weight, adapter_down_maps, adapter_up_maps, adapter_of_tile, cotangent):
    rows, width = tokens.shape
    feat = cotangent.shape[1]
    own, rank, _ = adapter_down_maps.shape
    tiles = rows // TILE
    hrank = rank // 2
    hrows = rows // 2
    srows = hrows // SUB
    dma = pltpu.SemaphoreType.DMA
    vm = pltpu.VMEM
    any_spec = pl.BlockSpec(memory_space=pl.ANY)
    vmem = pl.BlockSpec(memory_space=pltpu.VMEM)
    both = (feat, width)
    shapes = (
        jax.ShapeDtypeStruct((rows, feat), BF),
        jax.ShapeDtypeStruct((own, rank, width), F32),
        jax.ShapeDtypeStruct((own, rank, feat), F32),
    )

    def pair(dims, lead, kind):
        return [vm(lead + (dims, n), kind) for n in both]

    results = pl.pallas_call(
        kernel,
        out_shape=shapes,
        in_specs=[pl.BlockSpec(memory_space=pltpu.SMEM)] + [any_spec] * 5,
        out_specs=(vmem, vmem, vmem),
        scratch_shapes=[
            vm((rows, width), BF),
            vm((width, (NZ + 1) * feat), BF),
            vm((rows, feat), BF),
            *pair(rank, (2 * NC * 4 * 4 * 2,), BF),
            vm((2, 2, 2, hrows, feat), F32),
            vm((2, NZ - 1, SUB, srows, feat), BF),
            vm((2, NZ - 1, SUB, srows, feat), BF),
            vm((2, NZ, tiles // NZ, rank, TILE), BF),
            vm((2, NZ, tiles // NZ, rank, TILE), BF),
            vm((2, NZ, tiles // NZ, rank, TILE), BF),
            *pair(rank, (tiles + 1,), BF),
            *pair(hrank, (tiles + 1,), BF),
            vm((8, 128), jnp.int32),
            vm((8, 128), jnp.int32),
            pltpu.SMEM((2, 8, 128), jnp.int32),
            pltpu.SMEM((tiles,), jnp.int32),
            *pair(hrank, (2, 4, 2, 8), BF),
            *pair(hrank, (2, 2, 8), BF),
            *pair(hrank, (2, 2, 2, 8), BF),
            *pair(hrank, (2, 2, 8), F32),
            *pair(hrank, (2, 2, 8), BF),
            *pair(hrank, (2, 2, 2), BF),
            *pair(hrank, (2, 2, 2, 2), BF),
            *pair(hrank, (2, 2), F32),
            *pair(hrank, (2, 2), F32),
            dma((8 + NZ + 1,)),
            dma((2, 2, 5, 2)),
            dma((2, 2, 5, 2)),
            dma((2, 2, 4)),
            dma((2, 2, 4)),
            dma((2, NZ - 1, SUB)),
            dma((2, NZ - 1, SUB)),
            dma((2, NZ)),
            dma((2, NZ)),
            dma((2, NZ)),
            dma((2, NZ)),
            dma((3,)),
            dma((3,)),
            dma((2, 2, 2, 3, 2)),
            dma((2, 2, 2, 3, 2)),
            dma((2, 2, 3, 2)),
            dma((2, 2, 3, 2)),
            dma((2, 2)),
            dma((2, 2)),
        ],
        compiler_params=pltpu.CompilerParams(
            collective_id=0, has_side_effects=True, vmem_limit_bytes=56 * 2**20
        ),
        name="adapters_and_projection",
    )(adapter_of_tile, tokens, value_weight, adapter_down_maps, adapter_up_maps, cotangent)
    return pl.pallas_call(
        place,
        out_shape=shapes,
        in_specs=[vmem] * 3,
        out_specs=(vmem,) * 3,
        name="place_results",
    )(*results)


def solution(mesh):
    in_specs = (
        P("seq", "tensor"),
        P("tensor", None),
        P("seq", None, "tensor"),
        P("seq", None, "tensor"),
        P("seq"),
        P("seq", "tensor"),
    )
    out_specs = (P("seq", "tensor"), P("seq", None, "tensor"), P("seq", None, "tensor"))
    return jax.shard_map(body, mesh=mesh, in_specs=in_specs, out_specs=out_specs, check_vma=False)
```

```python
import jax
import jax.numpy as jnp
from jax import lax
from jax.experimental import pallas as pl
from jax.experimental.pallas import tpu as pltpu
from jax.sharding import PartitionSpec as P

TILE = 128
NX, NY, NC, NZ = 4, 4, 2, 8
OWN = 4
SCALE = 2.0
SUB = 2
BLK = 256
UN = 4
MESH = pl.DeviceIdType.MESH
BF = jnp.bfloat16
F32 = jnp.float32
DIRS = ((0, 1), (1, -1))
UP, DOWN = 0, 1
ALL_Q = ((0, 4),)
TWO_Q = ((0, 2), (2, 2))


def kernel(
    ids, tok_h, w_h, down_h, up_h, cot_h,
    val_o, gd_o, ug_o,
    tok, w, cot, adu, add, acc, zs, zr, part, ar, low, tu, td, tpu, tpd, tab, tabp, tabs, place_of,
    gu, gd, r1u, r1d, r2d, sfu, sfd, sbu, sbd, r3u, r3d, r4d, finu, find, rfu, rfd,
    lsem, ag_s, ag_r, d_s, d_r, z_s, z_r, ar_s, ar_r, br_s, br_r, t_s, t_r,
    g_s, g_r, q_s, q_r, f_s, f_r,
):
    width = tok.shape[1]
    rows = tok.shape[0]
    rank = down_h.shape[1]
    feat = cot.shape[1]
    tiles = rows // TILE
    hrank = rank // 2
    hrows = rows // 2
    srows = hrows // SUB
    ad = (adu, add)
    tt = (tu, td)
    tp = (tpu, tpd)
    g = (gu, gd)
    r1 = (r1u, r1d)
    r2 = (None, r2d)
    sf = (sfu, sfd)
    sb = (sbu, sbd)
    r3 = (r3u, r3d)
    r4 = (None, r4d)
    fin = (finu, find)
    rf = (rfu, rfd)
    out = (ug_o, gd_o)
    s_idx = lax.axis_index("seq")
    z = lax.axis_index("tensor")
    c = s_idx % 2
    x = (s_idx // 2) % NX
    y = s_idx // (2 * NX)
    pos = ((y, x), (x, y))

    def dev(yy, xx, cc):
        return ((yy * NX + xx) * NC + cc, z)

    def zdev(d):
        return (s_idx, (z + d) % NZ)

    def hdev(h, dp, dq):
        pp, qq = (pos[h][0] + dp + 4) % 4, (pos[h][1] + dq + 4) % 4
        return dev(pp, qq, c) if h == 0 else dev(qq, pp, c)

    mate = dev(y, x, 1 - c)

    def remote(src, dst, ss, rs, device):
        return pltpu.make_async_remote_copy(
            src_ref=src, dst_ref=dst, send_sem=ss, recv_sem=rs, device_id=device, device_id_type=MESH
        )

    sent = []

    def send(src, dst, ss, rs, device):
        cp = remote(src, dst, ss, rs, device)
        cp.start()
        sent.append(cp)

    def got(dst, ss, rs):
        remote(dst, dst, ss, rs, mate).wait_recv()

    def slot(h, side, p, q=0, k=0, n=1):
        return pl.ds((((h * 2 + side) * 4 + p) * 4 + q) * 2 + k, n)

    loads = []
    for h in range(2):
        loads.append(pltpu.make_async_copy(up_h.at[pl.ds(2 * h, 2)], adu.at[slot(h, 0, 0, n=2)], lsem.at[2 * h]))
        loads.append(pltpu.make_async_copy(down_h.at[pl.ds(2 * h, 2)], add.at[slot(h, 0, 0, n=2)], lsem.at[2 * h + 1]))
    loads.append(pltpu.make_async_copy(tok_h, tok, lsem.at[4]))
    loads.append(pltpu.make_async_copy(cot_h, cot, lsem.at[5]))
    for j in range(NZ + 1):
        d = (z + NZ - j) % NZ
        loads.append(
            pltpu.make_async_copy(
                w_h.at[:, pl.ds(pl.multiple_of(d * feat, feat), feat)],
                w.at[:, pl.ds(j * feat, feat)],
                lsem.at[8 + j],
            )
        )
    for cp in loads:
        cp.start()
    bar = pltpu.get_barrier_semaphore()
    friends = [zdev(d) for d in range(1, NZ)] + [mate]
    friends += [hdev(0, d, 0) for d in (1, 2, 3)] + [hdev(0, 0, d) for d in (1, 2, 3)]
    for f in friends:
        pl.semaphore_signal(bar, inc=1, device_id=f, device_id_type=MESH)
    lane = lax.broadcasted_iota(jnp.int32, (8, 128), 1)
    lane_h = lane // 64
    lane_p = (lane // 16) % 4
    lane_q = (lane // 2) % 4
    lane_q = jnp.where(lane_q == 0, 2, jnp.where(lane_q == 1, 1, jnp.where(lane_q == 2, 3, 0)))
    lane_y = (y + jnp.where(lane_h == 0, lane_p, lane_q)) % 4
    lane_x = (x + jnp.where(lane_h == 0, lane_q, lane_p)) % 4
    lane_c = (lane // 8 + c) % 2
    named = ((lane_y * NX + lane_x) * NC + lane_c) * OWN + 2 * lane_h + lane % 2
    row = lax.broadcasted_iota(jnp.int32, (8, 128), 0)
    first = jnp.full((8, 128), tiles, jnp.int32)
    count = jnp.zeros((8, 128), jnp.int32)
    last = jnp.full((8, 128), tiles, jnp.int32)
    for t in range(tiles):
        hit = named == ids[t]
        last = jnp.where(hit & (count == 1), t, last)
        first = jnp.where(hit & (count == 0), t, first)
        count = count + hit.astype(jnp.int32)
    tab[...] = jnp.where(row == 0, first, last)
    for e in range(2):
        tt[e][tiles] = jnp.zeros(tt[e].shape[1:], BF)
        tp[e][tiles] = jnp.zeros(tp[e].shape[1:], BF)
    for t in range(tiles):
        a = ids[t]
        owner = a // OWN
        h = (a % OWN) // 2
        xx = (owner // 2 + NX - x) % NX
        yy = (owner // (2 * NX) + NY - y) % NY
        pq = jnp.where(h == 0, yy * 4 + xx, xx * 4 + yy)
        place_of[t] = ((h * 2 + (owner + c) % 2) * 16 + pq) * 2 + a % 2
    for cp in loads[:4]:
        cp.wait()
    pl.semaphore_wait(bar, len(friends))

    def upq():
        for h in range(2):
            own = adu.at[slot(h, 0, 0, n=2)]
            for d in (1, 3, 2):
                send(
                    own, adu.at[slot(h, 0, 0, 4 - d, n=2)],
                    ag_s.at[UP, h, d, 0], ag_r.at[UP, h, d, 0], hdev(h, 0, d),
                )

    def upp():
        for h in range(2):
            for d in (1, 3, 2):
                got(adu.at[slot(h, 0, 0, 4 - d, n=2)], ag_s.at[UP, h, d, 0], ag_r.at[UP, h, d, 0])
            for d in (2, 1, 3):
                send(
                    adu.at[slot(h, 0, 0, n=8)], adu.at[slot(h, 0, 4 - d, n=8)],
                    ag_s.at[UP, h, d, 1], ag_r.at[UP, h, d, 1], hdev(h, d, 0),
                )
        for h in range(2):
            send(adu.at[slot(h, 0, 0, n=8)], adu.at[slot(h, 1, 0, n=8)], d_s.at[UP, h, 0], d_r.at[UP, h, 0], mate)

    def upd():
        for d in (1, 3, 2):
            for h in range(2):
                got(adu.at[slot(h, 0, 4 - d, n=8)], ag_s.at[UP, h, d, 1], ag_r.at[UP, h, d, 1])
                send(
                    adu.at[slot(h, 0, 4 - d, n=8)], adu.at[slot(h, 1, 4 - d, n=8)],
                    d_s.at[UP, h, 4 - d], d_r.at[UP, h, 4 - d], mate,
                )

    def ag1(e):
        for h in range(2):
            own = ad[e].at[slot(h, 0, 0, n=2)]
            for i, dq in DIRS:
                send(own, ad[e].at[slot(h, 0, 0, 3 - 2 * i, n=2)], ag_s.at[e, h, 0, i], ag_r.at[e, h, 0, i], hdev(h, 0, dq))

    def ag1p(e):
        for h in range(2):
            own = ad[e].at[slot(h, 0, 0, n=2)]
            for i, dp in DIRS:
                send(own, ad[e].at[slot(h, 0, 3 - 2 * i, n=2)], ag_s.at[e, h, 4, i], ag_r.at[e, h, 4, i], hdev(h, dp, 0))

    def ag2(e):
        for h in range(2):
            for i, dq in DIRS:
                near = 3 - 2 * i
                got(ad[e].at[slot(h, 0, 0, near, n=2)], ag_s.at[e, h, 0, i], ag_r.at[e, h, 0, i])
                send(
                    ad[e].at[slot(h, 0, 0, near, i)], ad[e].at[slot(h, 0, 0, 2, i)],
                    ag_s.at[e, h, 1, i], ag_r.at[e, h, 1, i], hdev(h, 0, dq),
                )

    def ag3(e):
        for h in range(2):
            for i, dq in DIRS:
                got(ad[e].at[slot(h, 0, 0, 2, i)], ag_s.at[e, h, 1, i], ag_r.at[e, h, 1, i])
            for i, dp in DIRS:
                send(
                    ad[e].at[slot(h, 0, 0, 1, n=6)], ad[e].at[slot(h, 0, 3 - 2 * i, 1, n=6)],
                    ag_s.at[e, h, 2, i], ag_r.at[e, h, 2, i], hdev(h, dp, 0),
                )
            send(ad[e].at[slot(h, 0, 0, n=8)], ad[e].at[slot(h, 1, 0, n=8)], d_s.at[e, h, 0], d_r.at[e, h, 0], mate)

    def ag4(e):
        for h in range(2):
            for i, dp in DIRS:
                near = 3 - 2 * i
                got(ad[e].at[slot(h, 0, near, n=2)], ag_s.at[e, h, 4, i], ag_r.at[e, h, 4, i])
                got(ad[e].at[slot(h, 0, near, 1, n=6)], ag_s.at[e, h, 2, i], ag_r.at[e, h, 2, i])
                send(
                    ad[e].at[slot(h, 0, near, 2 * i, n=4)], ad[e].at[slot(h, 0, 2, 2 * i, n=4)],
                    ag_s.at[e, h, 3, i], ag_r.at[e, h, 3, i], hdev(h, dp, 0),
                )
                send(ad[e].at[slot(h, 0, near, n=8)], ad[e].at[slot(h, 1, near, n=8)], d_s.at[e, h, near], d_r.at[e, h, near], mate)

    def ag5(e):
        for h in range(2):
            for i, dp in DIRS:
                got(ad[e].at[slot(h, 0, 2, 2 * i, n=4)], ag_s.at[e, h, 3, i], ag_r.at[e, h, 3, i])
            send(ad[e].at[slot(h, 0, 2, n=8)], ad[e].at[slot(h, 1, 2, n=8)], d_s.at[e, h, 2], d_r.at[e, h, 2], mate)

    def ag6(e):
        for h in range(2):
            for j in range(4):
                got(ad[e].at[slot(h, 1, j, n=8)], d_s.at[e, h, j], d_r.at[e, h, j])

    def zpart(m):
        for i in range(2):
            start = (2 * m + 1) * feat if i == 0 else (6 - 2 * m) * feat

            def step(r, _):
                rr = pl.ds(pl.multiple_of(r * BLK, BLK), BLK)
                a = tok[pl.ds(pl.multiple_of(i * hrows + r * BLK, BLK), BLK), :]
                v = jnp.dot(a, w[:, start : start + 2 * feat], preferred_element_type=F32)
                acc[m % 2, i, i, rr, :] = v[:, :feat]
                acc[m % 2, i, 1 - i, rr, :] = v[:, feat:]
                return 0

            lax.fori_loop(0, hrows // BLK, step, 0)

    def zsend(s, u):
        for i in range(2):
            if s > 0:
                got(zr.at[i, s - 1, u], z_s.at[i, s - 1, u], z_r.at[i, s - 1, u])

            def step(r, _):
                rr = pl.ds(pl.multiple_of(r * 128, 128), 128)
                v = acc[(s // 2) % 2, i, s % 2, pl.ds(pl.multiple_of(u * srows + r * 128, 128), 128), :]
                if s > 0:
                    v = v + zr[i, s - 1, u, rr, :].astype(F32)
                zs[i, s, u, rr, :] = v.astype(BF)
                return 0

            lax.fori_loop(0, srows // 128, step, 0)
            send(
                zs.at[i, s, u], zr.at[i, s, u], z_s.at[i, s, u], z_r.at[i, s, u],
                zdev(1) if i == 0 else zdev(NZ - 1),
            )

    def zlast(u):
        last_step = NZ - 2
        for i in range(2):
            got(zr.at[i, last_step, u], z_s.at[i, last_step, u], z_r.at[i, last_step, u])

            def step(r, _):
                t = (i * hrows + u * srows) // TILE + r
                rr = pl.ds(pl.multiple_of(r * TILE, TILE), TILE)
                v = acc[1, i, 1, pl.ds(pl.multiple_of(u * srows + r * TILE, TILE), TILE), :]
                v = v + zr[i, last_step, u, rr, :].astype(F32)
                upd = SCALE * lax.dot_general(
                    low[DOWN, t // 2, t % 2], adu[place_of[t]], (((0,), (0,)), ((), ())),
                    preferred_element_type=F32,
                )
                v = v + upd.astype(BF).astype(F32)
                val_o[pl.ds(pl.multiple_of(t * TILE, TILE), TILE), :] = v.astype(BF)
                return 0

            lax.fori_loop(0, srows // TILE, step, 0, unroll=UN)

    def lowpart(e):
        source = (cot, tok)[e]

        def step(t, _):
            rr = pl.ds(pl.multiple_of(t * TILE, TILE), TILE)
            v = lax.dot_general(
                ad[e][place_of[t]], source[rr, :], (((1,), (1,)), ((), ())), preferred_element_type=F32
            )
            part[e, t // 2, t % 2] = v.astype(BF)
            return 0

        lax.fori_loop(0, tiles, step, 0, unroll=UN)

    ORDER = (4, 3, 5, 2, 6, 1, 7)

    def arsend(e):
        lowpart(e)
        for d in ORDER:
            send(part.at[e, (z + d) % NZ], ar.at[e, d], ar_s.at[e, d], ar_r.at[e, d], zdev(d))

    def arsum(e):
        for d in range(1, NZ):
            got(ar.at[e, d], ar_s.at[e, d], ar_r.at[e, d])
        tot = part[e, z].astype(F32)
        for d in range(1, NZ):
            tot = tot + ar[e, d].astype(F32)
        if e == UP:
            tot = SCALE * tot
        low[e, z] = tot.astype(BF)
        for d in ORDER:
            send(low.at[e, z], low.at[e, z], br_s.at[e, d], br_r.at[e, d], zdev(d))

    def argot(e):
        for d in range(1, NZ):
            got(low.at[e, (z + NZ - d) % NZ], br_s.at[e, d], br_r.at[e, d])

    mine = pl.ds(pl.multiple_of(c * hrank, hrank), hrank)
    theirs = pl.ds(pl.multiple_of((1 - c) * hrank, hrank), hrank)

    def terms(e):
        source = (cot, tok)[e]

        def step(t, _):
            rr = pl.ds(pl.multiple_of(t * TILE, TILE), TILE)
            v = jnp.dot(low[1 - e, t // 2, t % 2], source[rr, :], preferred_element_type=F32)
            if e == UP:
                v = SCALE * v
            tt[e][t] = v.astype(BF)
            return 0

        lax.fori_loop(0, tiles, step, 0, unroll=UN)
        send(tt[e].at[pl.ds(0, tiles), theirs, :], tp[e].at[pl.ds(0, tiles)], t_s.at[e], t_r.at[e], mate)

    def tgot(e):
        got(tp[e].at[pl.ds(0, tiles)], t_s.at[e], t_r.at[e])

    def tables():
        cp = pltpu.make_async_copy(tab, tabs.at[0], lsem.at[6])
        cp.start()
        cp.wait()
        got(tabp, t_s.at[2], t_r.at[2])
        cp = pltpu.make_async_copy(tabp, tabs.at[1], lsem.at[7])
        cp.start()
        cp.wait()

    def build(e, h, rel, group):
        q0, n = group
        base = (h * 4 + rel) * 16
        for cc in range(2):
            here = base + cc * 8 + 2 * q0
            there = base + (1 - cc) * 8 + 2 * q0

            def step(j, _):
                v = tt[e][tabs[0, 0, here + j], mine, :].astype(F32)
                v = v + tt[e][tabs[0, 1, here + j], mine, :].astype(F32)
                v = v + tp[e][tabs[1, 0, there + j]].astype(F32)
                v = v + tp[e][tabs[1, 1, there + j]].astype(F32)
                g[e][h, rel, cc, 2 * q0 + j] = v.astype(BF)
                return 0

            lax.fori_loop(0, 2 * n, step, 0, unroll=min(UN, 2 * n))

    NEAR = (1, 3)

    def rs1far(e, groups, gi):
        q0, n = groups[gi]
        qs = pl.ds(2 * q0, 2 * n)
        for h in range(2):
            build(e, h, 2, groups[gi])
            for i, dp in DIRS:
                send(
                    g[e].at[h, 2, i, qs], r1[e].at[h, i, qs],
                    g_s.at[e, h, gi, 0, i], g_r.at[e, h, gi, 0, i], hdev(h, dp, 0),
                )

    def rs1near(e, groups, gi):
        q0, n = groups[gi]
        qs = pl.ds(2 * q0, 2 * n)
        for h in range(2):
            for i, dp in DIRS:
                build(e, h, NEAR[i], groups[gi])
                send(
                    g[e].at[h, NEAR[i], 1 - i, qs], r2[e].at[h, i, 1 - i, qs],
                    g_s.at[e, h, gi, 1, i], g_r.at[e, h, gi, 1, i], hdev(h, dp, 0),
                )

    def rs2(e, groups, gi):
        q0, n = groups[gi]
        qs = pl.ds(2 * q0, 2 * n)
        for h in range(2):
            for i, dp in DIRS:
                got(r1[e].at[h, i, qs], g_s.at[e, h, gi, 0, i], g_r.at[e, h, gi, 0, i])

                def step(j, _):
                    v = g[e][h, NEAR[i], i, 2 * q0 + j].astype(F32) + r1[e][h, i, 2 * q0 + j].astype(F32)
                    g[e][h, NEAR[i], i, 2 * q0 + j] = v.astype(BF)
                    return 0

                lax.fori_loop(0, 2 * n, step, 0, unroll=UN)
                send(
                    g[e].at[h, NEAR[i], i, qs], r2[e].at[h, i, i, qs],
                    g_s.at[e, h, gi, 2, i], g_r.at[e, h, gi, 2, i], hdev(h, dp, 0),
                )

    def rs3(e):
        for h in range(2):
            build(e, h, 0, (0, 4))

    def rs4(e, groups, gi):
        q0, n = groups[gi]
        qs = pl.ds(2 * q0, 2 * n)
        for h in range(2):
            for i, dp in DIRS:
                got(r2[e].at[h, i, 1 - i, qs], g_s.at[e, h, gi, 1, i], g_r.at[e, h, gi, 1, i])
                got(r2[e].at[h, i, i, qs], g_s.at[e, h, gi, 2, i], g_r.at[e, h, gi, 2, i])
            for cc in range(2):

                def step(j, _):
                    qk = 2 * q0 + j
                    v = g[e][h, 0, cc, qk].astype(F32) + r2[e][h, 0, cc, qk].astype(F32)
                    v = v + r2[e][h, 1, cc, qk].astype(F32)
                    sf[e][h, cc, qk] = v
                    sb[e][h, cc, qk] = v.astype(BF)
                    return 0

                lax.fori_loop(0, 2 * n, step, 0, unroll=UN)
            for i, dq in DIRS:
                if q0 == 0:
                    send(
                        sb[e].at[h, i, pl.ds(0, 2)], r3[e].at[h, i],
                        q_s.at[e, h, 0, i], q_r.at[e, h, 0, i], hdev(h, 0, dq),
                    )
                if q0 <= 1 + i < q0 + n:
                    send(
                        sb[e].at[h, 1 - i, pl.ds(2 + 2 * i, 2)], r4[e].at[h, i, 1 - i],
                        q_s.at[e, h, 1, i], q_r.at[e, h, 1, i], hdev(h, 0, dq),
                    )

    def rs5(e):
        for h in range(2):
            for i, dq in DIRS:
                got(r3[e].at[h, i], q_s.at[e, h, 0, i], q_r.at[e, h, 0, i])
                unit = pl.ds(2 + 2 * i, 2)
                sb[e][h, i, unit] = (sf[e][h, i, unit] + r3[e][h, i].astype(F32)).astype(BF)
                send(
                    sb[e].at[h, i, unit], r4[e].at[h, i, i],
                    q_s.at[e, h, 2, i], q_r.at[e, h, 2, i], hdev(h, 0, dq),
                )

    def rs6(e):
        for h in range(2):
            for i, dq in DIRS:
                got(r4[e].at[h, i, 1 - i], q_s.at[e, h, 1, i], q_r.at[e, h, 1, i])
                got(r4[e].at[h, i, i], q_s.at[e, h, 2, i], q_r.at[e, h, 2, i])
            own = pl.ds(6, 2)
            fin[e][h] = sf[e][h, 1, own] + r4[e][h, 0, 1].astype(F32) + r4[e][h, 1, 1].astype(F32)
            send(fin[e].at[h], rf[e].at[h], f_s.at[e, h], f_r.at[e, h], mate)
            v = sf[e][h, 0, own] + r4[e][h, 0, 0].astype(F32) + r4[e][h, 1, 0].astype(F32)
            out[e][pl.ds(2 * h, 2), mine, :] = v

    def rs7(e):
        for h in range(2):
            got(rf[e].at[h], f_s.at[e, h], f_r.at[e, h])
            out[e][pl.ds(2 * h, 2), theirs, :] = rf[e][h]

    def us1():
        for h in range(2):
            for d in (2, 1, 3):
                build(UP, h, d, (0, 4))
                send(
                    gu.at[h, d], r1u.at[h, d - 1],
                    g_s.at[UP, h, 0, d - 1, 0], g_r.at[UP, h, 0, d - 1, 0], hdev(h, d, 0),
                )
        for h in range(2):
            build(UP, h, 0, (0, 4))

    def us2():
        for h in range(2):
            for d in (1, 3, 2):
                got(r1u.at[h, d - 1], g_s.at[UP, h, 0, d - 1, 0], g_r.at[UP, h, 0, d - 1, 0])
            for cc in range(2):

                def step(j, _):
                    v = gu[h, 0, cc, j].astype(F32) + r1u[h, 0, cc, j].astype(F32)
                    v = v + r1u[h, 1, cc, j].astype(F32) + r1u[h, 2, cc, j].astype(F32)
                    sfu[h, cc, j] = v
                    sbu[h, cc, j] = v.astype(BF)
                    return 0

                lax.fori_loop(0, 8, step, 0, unroll=UN)
            for qi, d in enumerate((2, 1, 3)):
                send(
                    sbu.at[h, :, pl.ds(2 * qi, 2)], r3u.at[h, qi],
                    q_s.at[UP, h, qi, 0], q_r.at[UP, h, qi, 0], hdev(h, 0, d),
                )

    def us3():
        own = pl.ds(6, 2)
        for h in range(2):
            for qi in range(3):
                got(r3u.at[h, qi], q_s.at[UP, h, qi, 0], q_r.at[UP, h, qi, 0])
            v = sfu[h, 1, own]
            for qi in range(3):
                v = v + r3u[h, qi, 1].astype(F32)
            finu[h] = v
            send(finu.at[h], rfu.at[h], f_s.at[UP, h], f_r.at[UP, h], mate)
            v = sfu[h, 0, own]
            for qi in range(3):
                v = v + r3u[h, qi, 0].astype(F32)
            ug_o[pl.ds(2 * h, 2), mine, :] = v

    def tabsend():
        send(tab, tabp, t_s.at[2], t_r.at[2], mate)

    def landed(*which):
        for j in which:
            for cp in loads[j:] if j == 6 else loads[j : j + 1]:
                cp.wait()

    plan = (
        (upq,),
        (tabsend,),
        (ag1, DOWN),
        (landed, 4, 6),
        (zpart, 0),
        (zsend, 0, 0),
        (zsend, 0, 1),
        (upp,),
        (ag1p, DOWN),
        (ag2, DOWN),
        (landed, 5),
        (tables,),
        (upd,),
        (ag3, DOWN),
        (zsend, 1, 0),
        (ag6, UP),
        (arsend, UP),
        (zsend, 1, 1),
        (zpart, 1),
        (zsend, 2, 0),
        (arsum, UP),
        (ag4, DOWN),
        (zsend, 2, 1),
        (zpart, 2),
        (argot, UP),
        (terms, DOWN),
        (zsend, 3, 0),
        (ag5, DOWN),
        (zsend, 3, 1),
        (tgot, DOWN),
        (rs1far, DOWN, TWO_Q, 0),
        (rs1far, DOWN, TWO_Q, 1),
        (ag6, DOWN),
        (arsend, DOWN),
        (zsend, 4, 0),
        (rs1near, DOWN, TWO_Q, 0),
        (zsend, 4, 1),
        (rs1near, DOWN, TWO_Q, 1),
        (zpart, 3),
        (arsum, DOWN),
        (rs2, DOWN, TWO_Q, 0),
        (rs2, DOWN, TWO_Q, 1),
        (zsend, 5, 0),
        (zsend, 5, 1),
        (rs3, DOWN),
        (argot, DOWN),
        (terms, UP),
        (rs4, DOWN, TWO_Q, 0),
        (tgot, UP),
        (us1,),
        (zsend, 6, 0),
        (rs4, DOWN, TWO_Q, 1),
        (zsend, 6, 1),
        (rs5, DOWN),
        (us2,),
        (zlast, 0),
        (zlast, 1),
        (rs6, DOWN),
        (us3,),
        (rs7, DOWN),
        (rs7, UP),
    )
    for act, *details in plan:
        act(*details)
    for cp in sent:
        cp.wait_send()


def place(val_i, gd_i, ug_i, val_o, gd_o, ug_o):
    val_o[...] = val_i[...]
    gd_o[...] = gd_i[...]
    ug_o[...] = ug_i[...]


def body(tokens, value_weight, adapter_down_maps, adapter_up_maps, adapter_of_tile, cotangent):
    rows, width = tokens.shape
    feat = cotangent.shape[1]
    own, rank, _ = adapter_down_maps.shape
    tiles = rows // TILE
    hrank = rank // 2
    hrows = rows // 2
    srows = hrows // SUB
    dma = pltpu.SemaphoreType.DMA
    vm = pltpu.VMEM
    any_spec = pl.BlockSpec(memory_space=pl.ANY)
    vmem = pl.BlockSpec(memory_space=pltpu.VMEM)
    both = (feat, width)
    shapes = (
        jax.ShapeDtypeStruct((rows, feat), BF),
        jax.ShapeDtypeStruct((own, rank, width), F32),
        jax.ShapeDtypeStruct((own, rank, feat), F32),
    )

    def pair(dims, lead, kind):
        return [vm(lead + (dims, n), kind) for n in both]

    results = pl.pallas_call(
        kernel,
        out_shape=shapes,
        in_specs=[pl.BlockSpec(memory_space=pltpu.SMEM)] + [any_spec] * 5,
        out_specs=(vmem, vmem, vmem),
        scratch_shapes=[
            vm((rows, width), BF),
            vm((width, (NZ + 1) * feat), BF),
            vm((rows, feat), BF),
            *pair(rank, (2 * NC * 4 * 4 * 2,), BF),
            vm((2, 2, 2, hrows, feat), F32),
            vm((2, NZ - 1, SUB, srows, feat), BF),
            vm((2, NZ - 1, SUB, srows, feat), BF),
            vm((2, NZ, tiles // NZ, rank, TILE), BF),
            vm((2, NZ, tiles // NZ, rank, TILE), BF),
            vm((2, NZ, tiles // NZ, rank, TILE), BF),
            *pair(rank, (tiles + 1,), BF),
            *pair(hrank, (tiles + 1,), BF),
            vm((8, 128), jnp.int32),
            vm((8, 128), jnp.int32),
            pltpu.SMEM((2, 8, 128), jnp.int32),
            pltpu.SMEM((tiles,), jnp.int32),
            *pair(hrank, (2, 4, 2, 8), BF),
            vm((2, 3, 2, 8, hrank, feat), BF),
            vm((2, 2, 8, hrank, width), BF),
            vm((2, 2, 2, 8, hrank, width), BF),
            *pair(hrank, (2, 2, 8), F32),
            *pair(hrank, (2, 2, 8), BF),
            vm((2, 3, 2, 2, hrank, feat), BF),
            vm((2, 2, 2, hrank, width), BF),
            vm((2, 2, 2, 2, hrank, width), BF),
            *pair(hrank, (2, 2), F32),
            *pair(hrank, (2, 2), F32),
            dma((8 + NZ + 1,)),
            dma((2, 2, 5, 2)),
            dma((2, 2, 5, 2)),
            dma((2, 2, 4)),
            dma((2, 2, 4)),
            dma((2, NZ - 1, SUB)),
            dma((2, NZ - 1, SUB)),
            dma((2, NZ)),
            dma((2, NZ)),
            dma((2, NZ)),
            dma((2, NZ)),
            dma((3,)),
            dma((3,)),
            dma((2, 2, 2, 3, 2)),
            dma((2, 2, 2, 3, 2)),
            dma((2, 2, 3, 2)),
            dma((2, 2, 3, 2)),
            dma((2, 2)),
            dma((2, 2)),
        ],
        compiler_params=pltpu.CompilerParams(
            collective_id=0, has_side_effects=True, vmem_limit_bytes=56 * 2**20
        ),
        name="adapters_and_projection",
    )(adapter_of_tile, tokens, value_weight, adapter_down_maps, adapter_up_maps, cotangent)
    return pl.pallas_call(
        place,
        out_shape=shapes,
        in_specs=[vmem] * 3,
        out_specs=(vmem,) * 3,
        name="place_results",
    )(*results)


def solution(mesh):
    in_specs = (
        P("seq", "tensor"),
        P("tensor", None),
        P("seq", None, "tensor"),
        P("seq", None, "tensor"),
        P("seq"),
        P("seq", "tensor"),
    )
    out_specs = (P("seq", "tensor"), P("seq", None, "tensor"), P("seq", None, "tensor"))
    return jax.shard_map(body, mesh=mesh, in_specs=in_specs, out_specs=out_specs, check_vma=False)
```

```python
import jax
import jax.numpy as jnp
from jax import lax
from jax.experimental import pallas as pl
from jax.experimental.pallas import tpu as pltpu
from jax.sharding import PartitionSpec as P

TILE = 128
NX, NY, NC, NZ = 4, 4, 2, 8
OWN = 4
SCALE = 2.0
SUB = 2
BLK = 256
UN = 4
MESH = pl.DeviceIdType.MESH
BF = jnp.bfloat16
F32 = jnp.float32
DIRS = ((0, 1), (1, -1))
UP, DOWN = 0, 1
ALL_Q = ((0, 4),)
TWO_Q = ((0, 2), (2, 2))


def kernel(
    ids, tok_h, w_h, down_h, up_h, cot_h,
    val_o, gd_o, ug_o,
    tok, w, cot, adu, add, acc, zs, zr, part, ar, low, tu, td, tpu, tpd, tab, tabp, tabs, place_of,
    gu, gd, r1u, r1d, r2d, sfu, sfd, sbu, sbd, r3u, r3d, r4d, finu, find, rfu, rfd,
    lsem, ag_s, ag_r, d_s, d_r, z_s, z_r, ar_s, ar_r, br_s, br_r, t_s, t_r,
    g_s, g_r, q_s, q_r, f_s, f_r,
):
    width = tok.shape[1]
    rows = tok.shape[0]
    rank = down_h.shape[1]
    feat = cot.shape[1]
    tiles = rows // TILE
    hrank = rank // 2
    hrows = rows // 2
    srows = hrows // SUB
    ad = (adu, add)
    tt = (tu, td)
    tp = (tpu, tpd)
    g = (gu, gd)
    r1 = (r1u, r1d)
    r2 = (None, r2d)
    sf = (sfu, sfd)
    sb = (sbu, sbd)
    r3 = (r3u, r3d)
    r4 = (None, r4d)
    fin = (finu, find)
    rf = (rfu, rfd)
    out = (ug_o, gd_o)
    s_idx = lax.axis_index("seq")
    z = lax.axis_index("tensor")
    c = s_idx % 2
    x = (s_idx // 2) % NX
    y = s_idx // (2 * NX)
    pos = ((y, x), (x, y))

    def dev(yy, xx, cc):
        return ((yy * NX + xx) * NC + cc, z)

    def zdev(d):
        return (s_idx, (z + d) % NZ)

    def hdev(h, dp, dq):
        pp, qq = (pos[h][0] + dp + 4) % 4, (pos[h][1] + dq + 4) % 4
        return dev(pp, qq, c) if h == 0 else dev(qq, pp, c)

    mate = dev(y, x, 1 - c)

    def remote(src, dst, ss, rs, device):
        return pltpu.make_async_remote_copy(
            src_ref=src, dst_ref=dst, send_sem=ss, recv_sem=rs, device_id=device, device_id_type=MESH
        )

    sent = []

    def send(src, dst, ss, rs, device):
        cp = remote(src, dst, ss, rs, device)
        cp.start()
        sent.append(cp)

    def got(dst, ss, rs):
        remote(dst, dst, ss, rs, mate).wait_recv()

    def slot(h, side, p, q=0, k=0, n=1):
        return pl.ds((((h * 2 + side) * 4 + p) * 4 + q) * 2 + k, n)

    loads = []
    for h in range(2):
        loads.append(pltpu.make_async_copy(up_h.at[pl.ds(2 * h, 2)], adu.at[slot(h, 0, 0, n=2)], lsem.at[2 * h]))
        loads.append(pltpu.make_async_copy(down_h.at[pl.ds(2 * h, 2)], add.at[slot(h, 0, 0, n=2)], lsem.at[2 * h + 1]))
    loads.append(pltpu.make_async_copy(tok_h, tok, lsem.at[4]))
    loads.append(pltpu.make_async_copy(cot_h, cot, lsem.at[5]))
    for j in range(NZ + 1):
        d = (z + NZ - j) % NZ
        loads.append(
            pltpu.make_async_copy(
                w_h.at[:, pl.ds(pl.multiple_of(d * feat, feat), feat)],
                w.at[:, pl.ds(j * feat, feat)],
                lsem.at[8 + j],
            )
        )
    for cp in loads:
        cp.start()
    bar = pltpu.get_barrier_semaphore()
    friends = [zdev(d) for d in range(1, NZ)] + [mate]
    friends += [hdev(0, d, 0) for d in (1, 2, 3)] + [hdev(0, 0, d) for d in (1, 2, 3)]
    for f in friends:
        pl.semaphore_signal(bar, inc=1, device_id=f, device_id_type=MESH)
    lane = lax.broadcasted_iota(jnp.int32, (8, 128), 1)
    lane_h = lane // 64
    lane_p = (lane // 16) % 4
    lane_q = (lane // 2) % 4
    lane_q = jnp.where(lane_q == 0, 2, jnp.where(lane_q == 1, 1, jnp.where(lane_q == 2, 3, 0)))
    lane_y = (y + jnp.where(lane_h == 0, lane_p, lane_q)) % 4
    lane_x = (x + jnp.where(lane_h == 0, lane_q, lane_p)) % 4
    lane_c = (lane // 8 + c) % 2
    named = ((lane_y * NX + lane_x) * NC + lane_c) * OWN + 2 * lane_h + lane % 2
    row = lax.broadcasted_iota(jnp.int32, (8, 128), 0)
    first = jnp.full((8, 128), tiles, jnp.int32)
    count = jnp.zeros((8, 128), jnp.int32)
    last = jnp.full((8, 128), tiles, jnp.int32)
    for t in range(tiles):
        hit = named == ids[t]
        last = jnp.where(hit & (count == 1), t, last)
        first = jnp.where(hit & (count == 0), t, first)
        count = count + hit.astype(jnp.int32)
    tab[...] = jnp.where(row == 0, first, last)
    for e in range(2):
        tt[e][tiles] = jnp.zeros(tt[e].shape[1:], BF)
        tp[e][tiles] = jnp.zeros(tp[e].shape[1:], BF)
    for t in range(tiles):
        a = ids[t]
        owner = a // OWN
        h = (a % OWN) // 2
        xx = (owner // 2 + NX - x) % NX
        yy = (owner // (2 * NX) + NY - y) % NY
        pq = jnp.where(h == 0, yy * 4 + xx, xx * 4 + yy)
        place_of[t] = ((h * 2 + (owner + c) % 2) * 16 + pq) * 2 + a % 2
    for cp in loads[:4]:
        cp.wait()
    pl.semaphore_wait(bar, len(friends))

    def upq():
        for h in range(2):
            own = adu.at[slot(h, 0, 0, n=2)]
            for d in (1, 3, 2):
                send(
                    own, adu.at[slot(h, 0, 0, 4 - d, n=2)],
                    ag_s.at[UP, h, d, 0], ag_r.at[UP, h, d, 0], hdev(h, 0, d),
                )

    def upp():
        for h in range(2):
            for d in (1, 3, 2):
                got(adu.at[slot(h, 0, 0, 4 - d, n=2)], ag_s.at[UP, h, d, 0], ag_r.at[UP, h, d, 0])
            for d in (2, 1, 3):
                send(
                    adu.at[slot(h, 0, 0, n=8)], adu.at[slot(h, 0, 4 - d, n=8)],
                    ag_s.at[UP, h, d, 1], ag_r.at[UP, h, d, 1], hdev(h, d, 0),
                )
        for h in range(2):
            send(adu.at[slot(h, 0, 0, n=8)], adu.at[slot(h, 1, 0, n=8)], d_s.at[UP, h, 0], d_r.at[UP, h, 0], mate)

    def upd():
        for d in (1, 3, 2):
            for h in range(2):
                got(adu.at[slot(h, 0, 4 - d, n=8)], ag_s.at[UP, h, d, 1], ag_r.at[UP, h, d, 1])
                send(
                    adu.at[slot(h, 0, 4 - d, n=8)], adu.at[slot(h, 1, 4 - d, n=8)],
                    d_s.at[UP, h, 4 - d], d_r.at[UP, h, 4 - d], mate,
                )

    def ag1(e):
        for h in range(2):
            own = ad[e].at[slot(h, 0, 0, n=2)]
            for i, dq in DIRS:
                send(own, ad[e].at[slot(h, 0, 0, 3 - 2 * i, n=2)], ag_s.at[e, h, 0, i], ag_r.at[e, h, 0, i], hdev(h, 0, dq))

    def ag1p(e):
        for h in range(2):
            own = ad[e].at[slot(h, 0, 0, n=2)]
            for i, dp in DIRS:
                send(own, ad[e].at[slot(h, 0, 3 - 2 * i, n=2)], ag_s.at[e, h, 4, i], ag_r.at[e, h, 4, i], hdev(h, dp, 0))

    def ag2(e):
        for h in range(2):
            for i, dq in DIRS:
                near = 3 - 2 * i
                got(ad[e].at[slot(h, 0, 0, near, n=2)], ag_s.at[e, h, 0, i], ag_r.at[e, h, 0, i])
                send(
                    ad[e].at[slot(h, 0, 0, near, i)], ad[e].at[slot(h, 0, 0, 2, i)],
                    ag_s.at[e, h, 1, i], ag_r.at[e, h, 1, i], hdev(h, 0, dq),
                )

    def ag3(e):
        for h in range(2):
            for i, dq in DIRS:
                got(ad[e].at[slot(h, 0, 0, 2, i)], ag_s.at[e, h, 1, i], ag_r.at[e, h, 1, i])
            for i, dp in DIRS:
                send(
                    ad[e].at[slot(h, 0, 0, 1, n=6)], ad[e].at[slot(h, 0, 3 - 2 * i, 1, n=6)],
                    ag_s.at[e, h, 2, i], ag_r.at[e, h, 2, i], hdev(h, dp, 0),
                )
            send(ad[e].at[slot(h, 0, 0, n=8)], ad[e].at[slot(h, 1, 0, n=8)], d_s.at[e, h, 0], d_r.at[e, h, 0], mate)

    def ag4(e):
        for h in range(2):
            for i, dp in DIRS:
                near = 3 - 2 * i
                got(ad[e].at[slot(h, 0, near, n=2)], ag_s.at[e, h, 4, i], ag_r.at[e, h, 4, i])
                got(ad[e].at[slot(h, 0, near, 1, n=6)], ag_s.at[e, h, 2, i], ag_r.at[e, h, 2, i])
                send(
                    ad[e].at[slot(h, 0, near, 2 * i, n=4)], ad[e].at[slot(h, 0, 2, 2 * i, n=4)],
                    ag_s.at[e, h, 3, i], ag_r.at[e, h, 3, i], hdev(h, dp, 0),
                )
                send(ad[e].at[slot(h, 0, near, n=8)], ad[e].at[slot(h, 1, near, n=8)], d_s.at[e, h, near], d_r.at[e, h, near], mate)

    def ag5(e):
        for h in range(2):
            for i, dp in DIRS:
                got(ad[e].at[slot(h, 0, 2, 2 * i, n=4)], ag_s.at[e, h, 3, i], ag_r.at[e, h, 3, i])
            send(ad[e].at[slot(h, 0, 2, n=8)], ad[e].at[slot(h, 1, 2, n=8)], d_s.at[e, h, 2], d_r.at[e, h, 2], mate)

    def ag6(e):
        for h in range(2):
            for j in range(4):
                got(ad[e].at[slot(h, 1, j, n=8)], d_s.at[e, h, j], d_r.at[e, h, j])

    def zpart(m):
        for i in range(2):
            start = (2 * m + 1) * feat if i == 0 else (6 - 2 * m) * feat

            def step(r, _):
                rr = pl.ds(pl.multiple_of(r * BLK, BLK), BLK)
                a = tok[pl.ds(pl.multiple_of(i * hrows + r * BLK, BLK), BLK), :]
                v = jnp.dot(a, w[:, start : start + 2 * feat], preferred_element_type=F32)
                acc[m % 2, i, i, rr, :] = v[:, :feat]
                acc[m % 2, i, 1 - i, rr, :] = v[:, feat:]
                return 0

            lax.fori_loop(0, hrows // BLK, step, 0)

    def zsend(s, u):
        for i in range(2):
            if s > 0:
                got(zr.at[i, s - 1, u], z_s.at[i, s - 1, u], z_r.at[i, s - 1, u])

            def step(r, _):
                rr = pl.ds(pl.multiple_of(r * 128, 128), 128)
                v = acc[(s // 2) % 2, i, s % 2, pl.ds(pl.multiple_of(u * srows + r * 128, 128), 128), :]
                if s > 0:
                    v = v + zr[i, s - 1, u, rr, :].astype(F32)
                zs[i, s, u, rr, :] = v.astype(BF)
                return 0

            lax.fori_loop(0, srows // 128, step, 0)
            send(
                zs.at[i, s, u], zr.at[i, s, u], z_s.at[i, s, u], z_r.at[i, s, u],
                zdev(1) if i == 0 else zdev(NZ - 1),
            )

    def zlast(u):
        last_step = NZ - 2
        for i in range(2):
            got(zr.at[i, last_step, u], z_s.at[i, last_step, u], z_r.at[i, last_step, u])

            def step(r, _):
                t = (i * hrows + u * srows) // TILE + r
                rr = pl.ds(pl.multiple_of(r * TILE, TILE), TILE)
                v = acc[1, i, 1, pl.ds(pl.multiple_of(u * srows + r * TILE, TILE), TILE), :]
                v = v + zr[i, last_step, u, rr, :].astype(F32)
                upd = SCALE * lax.dot_general(
                    low[DOWN, t // 2, t % 2], adu[place_of[t]], (((0,), (0,)), ((), ())),
                    preferred_element_type=F32,
                )
                v = v + upd.astype(BF).astype(F32)
                val_o[pl.ds(pl.multiple_of(t * TILE, TILE), TILE), :] = v.astype(BF)
                return 0

            lax.fori_loop(0, srows // TILE, step, 0, unroll=UN)

    def lowpart(e):
        source = (cot, tok)[e]

        def step(t, _):
            rr = pl.ds(pl.multiple_of(t * TILE, TILE), TILE)
            v = lax.dot_general(
                ad[e][place_of[t]], source[rr, :], (((1,), (1,)), ((), ())), preferred_element_type=F32
            )
            part[e, t // 2, t % 2] = v.astype(BF)
            return 0

        lax.fori_loop(0, tiles, step, 0, unroll=UN)

    ORDER = (4, 3, 5, 2, 6, 1, 7)

    def arsend(e):
        lowpart(e)
        for d in ORDER:
            send(part.at[e, (z + d) % NZ], ar.at[e, d], ar_s.at[e, d], ar_r.at[e, d], zdev(d))

    def arsum(e):
        for d in range(1, NZ):
            got(ar.at[e, d], ar_s.at[e, d], ar_r.at[e, d])
        tot = part[e, z].astype(F32)
        for d in range(1, NZ):
            tot = tot + ar[e, d].astype(F32)
        if e == UP:
            tot = SCALE * tot
        low[e, z] = tot.astype(BF)
        for d in ORDER:
            send(low.at[e, z], low.at[e, z], br_s.at[e, d], br_r.at[e, d], zdev(d))

    def argot(e):
        for d in range(1, NZ):
            got(low.at[e, (z + NZ - d) % NZ], br_s.at[e, d], br_r.at[e, d])

    mine = pl.ds(pl.multiple_of(c * hrank, hrank), hrank)
    theirs = pl.ds(pl.multiple_of((1 - c) * hrank, hrank), hrank)

    def terms(e):
        source = (cot, tok)[e]

        def step(t, _):
            rr = pl.ds(pl.multiple_of(t * TILE, TILE), TILE)
            v = jnp.dot(low[1 - e, t // 2, t % 2], source[rr, :], preferred_element_type=F32)
            if e == UP:
                v = SCALE * v
            tt[e][t] = v.astype(BF)
            return 0

        lax.fori_loop(0, tiles, step, 0, unroll=UN)
        send(tt[e].at[pl.ds(0, tiles), theirs, :], tp[e].at[pl.ds(0, tiles)], t_s.at[e], t_r.at[e], mate)

    def tgot(e):
        got(tp[e].at[pl.ds(0, tiles)], t_s.at[e], t_r.at[e])

    def tables():
        cp = pltpu.make_async_copy(tab, tabs.at[0], lsem.at[6])
        cp.start()
        cp.wait()
        got(tabp, t_s.at[2], t_r.at[2])
        cp = pltpu.make_async_copy(tabp, tabs.at[1], lsem.at[7])
        cp.start()
        cp.wait()

    def build(e, h, rel, group):
        q0, n = group
        base = (h * 4 + rel) * 16
        for cc in range(2):
            here = base + cc * 8 + 2 * q0
            there = base + (1 - cc) * 8 + 2 * q0

            def step(j, _):
                v = tt[e][tabs[0, 0, here + j], mine, :].astype(F32)
                v = v + tt[e][tabs[0, 1, here + j], mine, :].astype(F32)
                v = v + tp[e][tabs[1, 0, there + j]].astype(F32)
                v = v + tp[e][tabs[1, 1, there + j]].astype(F32)
                g[e][h, rel, cc, 2 * q0 + j] = v.astype(BF)
                return 0

            lax.fori_loop(0, 2 * n, step, 0, unroll=min(UN, 2 * n))

    NEAR = (1, 3)

    def rs1far(e, groups, gi):
        q0, n = groups[gi]
        qs = pl.ds(2 * q0, 2 * n)
        for h in range(2):
            build(e, h, 2, groups[gi])
            for i, dp in DIRS:
                send(
                    g[e].at[h, 2, i, qs], r1[e].at[h, i, qs],
                    g_s.at[e, h, gi, 0, i], g_r.at[e, h, gi, 0, i], hdev(h, dp, 0),
                )

    def rs1near(e, groups, gi):
        q0, n = groups[gi]
        qs = pl.ds(2 * q0, 2 * n)
        for h in range(2):
            for i, dp in DIRS:
                build(e, h, NEAR[i], groups[gi])
                send(
                    g[e].at[h, NEAR[i], 1 - i, qs], r2[e].at[h, i, 1 - i, qs],
                    g_s.at[e, h, gi, 1, i], g_r.at[e, h, gi, 1, i], hdev(h, dp, 0),
                )

    def rs2(e, groups, gi):
        q0, n = groups[gi]
        qs = pl.ds(2 * q0, 2 * n)
        for h in range(2):
            for i, dp in DIRS:
                got(r1[e].at[h, i, qs], g_s.at[e, h, gi, 0, i], g_r.at[e, h, gi, 0, i])

                def step(j, _):
                    v = g[e][h, NEAR[i], i, 2 * q0 + j].astype(F32) + r1[e][h, i, 2 * q0 + j].astype(F32)
                    g[e][h, NEAR[i], i, 2 * q0 + j] = v.astype(BF)
                    return 0

                lax.fori_loop(0, 2 * n, step, 0, unroll=UN)
                send(
                    g[e].at[h, NEAR[i], i, qs], r2[e].at[h, i, i, qs],
                    g_s.at[e, h, gi, 2, i], g_r.at[e, h, gi, 2, i], hdev(h, dp, 0),
                )

    def rs3(e):
        for h in range(2):
            build(e, h, 0, (0, 4))

    def rs4(e, groups, gi):
        q0, n = groups[gi]
        qs = pl.ds(2 * q0, 2 * n)
        for h in range(2):
            for i, dp in DIRS:
                got(r2[e].at[h, i, 1 - i, qs], g_s.at[e, h, gi, 1, i], g_r.at[e, h, gi, 1, i])
                got(r2[e].at[h, i, i, qs], g_s.at[e, h, gi, 2, i], g_r.at[e, h, gi, 2, i])
            for cc in range(2):

                def step(j, _):
                    qk = 2 * q0 + j
                    v = g[e][h, 0, cc, qk].astype(F32) + r2[e][h, 0, cc, qk].astype(F32)
                    v = v + r2[e][h, 1, cc, qk].astype(F32)
                    sf[e][h, cc, qk] = v
                    sb[e][h, cc, qk] = v.astype(BF)
                    return 0

                lax.fori_loop(0, 2 * n, step, 0, unroll=UN)
            for i, dq in DIRS:
                if q0 == 0:
                    send(
                        sb[e].at[h, i, pl.ds(0, 2)], r3[e].at[h, i],
                        q_s.at[e, h, 0, i], q_r.at[e, h, 0, i], hdev(h, 0, dq),
                    )
                if q0 <= 1 + i < q0 + n:
                    send(
                        sb[e].at[h, 1 - i, pl.ds(2 + 2 * i, 2)], r4[e].at[h, i, 1 - i],
                        q_s.at[e, h, 1, i], q_r.at[e, h, 1, i], hdev(h, 0, dq),
                    )

    def rs5(e):
        for h in range(2):
            for i, dq in DIRS:
                got(r3[e].at[h, i], q_s.at[e, h, 0, i], q_r.at[e, h, 0, i])
                unit = pl.ds(2 + 2 * i, 2)
                sb[e][h, i, unit] = (sf[e][h, i, unit] + r3[e][h, i].astype(F32)).astype(BF)
                send(
                    sb[e].at[h, i, unit], r4[e].at[h, i, i],
                    q_s.at[e, h, 2, i], q_r.at[e, h, 2, i], hdev(h, 0, dq),
                )

    def rs6(e):
        for h in range(2):
            for i, dq in DIRS:
                got(r4[e].at[h, i, 1 - i], q_s.at[e, h, 1, i], q_r.at[e, h, 1, i])
                got(r4[e].at[h, i, i], q_s.at[e, h, 2, i], q_r.at[e, h, 2, i])
            own = pl.ds(6, 2)
            fin[e][h] = sf[e][h, 1, own] + r4[e][h, 0, 1].astype(F32) + r4[e][h, 1, 1].astype(F32)
            send(fin[e].at[h], rf[e].at[h], f_s.at[e, h], f_r.at[e, h], mate)
            v = sf[e][h, 0, own] + r4[e][h, 0, 0].astype(F32) + r4[e][h, 1, 0].astype(F32)
            out[e][pl.ds(2 * h, 2), mine, :] = v

    def rs7(e):
        for h in range(2):
            got(rf[e].at[h], f_s.at[e, h], f_r.at[e, h])
            out[e][pl.ds(2 * h, 2), theirs, :] = rf[e][h]

    def us1():
        for h in range(2):
            for d in (2, 1, 3):
                build(UP, h, d, (0, 4))
                send(
                    gu.at[h, d], r1u.at[h, d - 1],
                    g_s.at[UP, h, 0, d - 1, 0], g_r.at[UP, h, 0, d - 1, 0], hdev(h, d, 0),
                )
        for h in range(2):
            build(UP, h, 0, (0, 4))

    def us2():
        for h in range(2):
            for d in (1, 3, 2):
                got(r1u.at[h, d - 1], g_s.at[UP, h, 0, d - 1, 0], g_r.at[UP, h, 0, d - 1, 0])
            for cc in range(2):

                def step(j, _):
                    v = gu[h, 0, cc, j].astype(F32) + r1u[h, 0, cc, j].astype(F32)
                    v = v + r1u[h, 1, cc, j].astype(F32) + r1u[h, 2, cc, j].astype(F32)
                    sfu[h, cc, j] = v
                    sbu[h, cc, j] = v.astype(BF)
                    return 0

                lax.fori_loop(0, 8, step, 0, unroll=UN)
            for qi, d in enumerate((2, 1, 3)):
                send(
                    sbu.at[h, :, pl.ds(2 * qi, 2)], r3u.at[h, qi],
                    q_s.at[UP, h, qi, 0], q_r.at[UP, h, qi, 0], hdev(h, 0, d),
                )

    def us3():
        own = pl.ds(6, 2)
        for h in range(2):
            for qi in range(3):
                got(r3u.at[h, qi], q_s.at[UP, h, qi, 0], q_r.at[UP, h, qi, 0])
            v = sfu[h, 1, own]
            for qi in range(3):
                v = v + r3u[h, qi, 1].astype(F32)
            finu[h] = v
            send(finu.at[h], rfu.at[h], f_s.at[UP, h], f_r.at[UP, h], mate)
            v = sfu[h, 0, own]
            for qi in range(3):
                v = v + r3u[h, qi, 0].astype(F32)
            ug_o[pl.ds(2 * h, 2), mine, :] = v

    def tabsend():
        send(tab, tabp, t_s.at[2], t_r.at[2], mate)

    def landed(*which):
        for j in which:
            for cp in loads[j:] if j == 6 else loads[j : j + 1]:
                cp.wait()

    plan = (
        (upq,),
        (tabsend,),
        (ag1, DOWN),
        (landed, 4, 6),
        (zpart, 0),
        (upp,),
        (zsend, 0, 0),
        (zsend, 0, 1),
        (ag1p, DOWN),
        (ag2, DOWN),
        (landed, 5),
        (tables,),
        (upd,),
        (ag3, DOWN),
        (zsend, 1, 0),
        (ag6, UP),
        (arsend, UP),
        (zsend, 1, 1),
        (zpart, 1),
        (arsum, UP),
        (zsend, 2, 0),
        (ag4, DOWN),
        (zsend, 2, 1),
        (zpart, 2),
        (argot, UP),
        (zsend, 3, 0),
        (terms, DOWN),
        (ag5, DOWN),
        (zsend, 3, 1),
        (tgot, DOWN),
        (rs1far, DOWN, TWO_Q, 0),
        (rs1far, DOWN, TWO_Q, 1),
        (ag6, DOWN),
        (arsend, DOWN),
        (rs1near, DOWN, TWO_Q, 0),
        (zsend, 4, 0),
        (zsend, 4, 1),
        (rs1near, DOWN, TWO_Q, 1),
        (zpart, 3),
        (arsum, DOWN),
        (rs2, DOWN, TWO_Q, 0),
        (rs2, DOWN, TWO_Q, 1),
        (zsend, 5, 0),
        (zsend, 5, 1),
        (rs3, DOWN),
        (argot, DOWN),
        (terms, UP),
        (rs4, DOWN, TWO_Q, 0),
        (tgot, UP),
        (us1,),
        (zsend, 6, 0),
        (rs4, DOWN, TWO_Q, 1),
        (zsend, 6, 1),
        (rs5, DOWN),
        (us2,),
        (zlast, 0),
        (zlast, 1),
        (rs6, DOWN),
        (us3,),
        (rs7, DOWN),
        (rs7, UP),
    )
    for act, *details in plan:
        act(*details)
    for cp in sent:
        cp.wait_send()


def place(val_i, gd_i, ug_i, val_o, gd_o, ug_o):
    val_o[...] = val_i[...]
    gd_o[...] = gd_i[...]
    ug_o[...] = ug_i[...]


def body(tokens, value_weight, adapter_down_maps, adapter_up_maps, adapter_of_tile, cotangent):
    rows, width = tokens.shape
    feat = cotangent.shape[1]
    own, rank, _ = adapter_down_maps.shape
    tiles = rows // TILE
    hrank = rank // 2
    hrows = rows // 2
    srows = hrows // SUB
    dma = pltpu.SemaphoreType.DMA
    vm = pltpu.VMEM
    any_spec = pl.BlockSpec(memory_space=pl.ANY)
    vmem = pl.BlockSpec(memory_space=pltpu.VMEM)
    both = (feat, width)
    shapes = (
        jax.ShapeDtypeStruct((rows, feat), BF),
        jax.ShapeDtypeStruct((own, rank, width), F32),
        jax.ShapeDtypeStruct((own, rank, feat), F32),
    )

    def pair(dims, lead, kind):
        return [vm(lead + (dims, n), kind) for n in both]

    results = pl.pallas_call(
        kernel,
        out_shape=shapes,
        in_specs=[pl.BlockSpec(memory_space=pltpu.SMEM)] + [any_spec] * 5,
        out_specs=(vmem, vmem, vmem),
        scratch_shapes=[
            vm((rows, width), BF),
            vm((width, (NZ + 1) * feat), BF),
            vm((rows, feat), BF),
            *pair(rank, (2 * NC * 4 * 4 * 2,), BF),
            vm((2, 2, 2, hrows, feat), F32),
            vm((2, NZ - 1, SUB, srows, feat), BF),
            vm((2, NZ - 1, SUB, srows, feat), BF),
            vm((2, NZ, tiles // NZ, rank, TILE), BF),
            vm((2, NZ, tiles // NZ, rank, TILE), BF),
            vm((2, NZ, tiles // NZ, rank, TILE), BF),
            *pair(rank, (tiles + 1,), BF),
            *pair(hrank, (tiles + 1,), BF),
            vm((8, 128), jnp.int32),
            vm((8, 128), jnp.int32),
            pltpu.SMEM((2, 8, 128), jnp.int32),
            pltpu.SMEM((tiles,), jnp.int32),
            *pair(hrank, (2, 4, 2, 8), BF),
            vm((2, 3, 2, 8, hrank, feat), BF),
            vm((2, 2, 8, hrank, width), BF),
            vm((2, 2, 2, 8, hrank, width), BF),
            *pair(hrank, (2, 2, 8), F32),
            *pair(hrank, (2, 2, 8), BF),
            vm((2, 3, 2, 2, hrank, feat), BF),
            vm((2, 2, 2, hrank, width), BF),
            vm((2, 2, 2, 2, hrank, width), BF),
            *pair(hrank, (2, 2), F32),
            *pair(hrank, (2, 2), F32),
            dma((8 + NZ + 1,)),
            dma((2, 2, 5, 2)),
            dma((2, 2, 5, 2)),
            dma((2, 2, 4)),
            dma((2, 2, 4)),
            dma((2, NZ - 1, SUB)),
            dma((2, NZ - 1, SUB)),
            dma((2, NZ)),
            dma((2, NZ)),
            dma((2, NZ)),
            dma((2, NZ)),
            dma((3,)),
            dma((3,)),
            dma((2, 2, 2, 3, 2)),
            dma((2, 2, 2, 3, 2)),
            dma((2, 2, 3, 2)),
            dma((2, 2, 3, 2)),
            dma((2, 2)),
            dma((2, 2)),
        ],
        compiler_params=pltpu.CompilerParams(
            collective_id=0, has_side_effects=True, vmem_limit_bytes=56 * 2**20
        ),
        name="adapters_and_projection",
    )(adapter_of_tile, tokens, value_weight, adapter_down_maps, adapter_up_maps, cotangent)
    return pl.pallas_call(
        place,
        out_shape=shapes,
        in_specs=[vmem] * 3,
        out_specs=(vmem,) * 3,
        name="place_results",
    )(*results)


def solution(mesh):
    in_specs = (
        P("seq", "tensor"),
        P("tensor", None),
        P("seq", None, "tensor"),
        P("seq", None, "tensor"),
        P("seq"),
        P("seq", "tensor"),
    )
    out_specs = (P("seq", "tensor"), P("seq", None, "tensor"), P("seq", None, "tensor"))
    return jax.shard_map(body, mesh=mesh, in_specs=in_specs, out_specs=out_specs, check_vma=False)
```
